256 devices in a mesh: batch: 256 (over z, x, y, core).
Axes of the slice: x: 4, y: 4, z: 8, core: 2. Of those that a mesh axis runs over, the one named last changes fastest.
Arguments:
- img_emb: bfloat16 [131072, 1152], P('batch'), may hold values from -0.19921875 to 0.19921875
- txt_feat: bfloat16 [131072, 1152], P('batch'), may hold values from -0.19921875 to 0.19921875
- txt_head: bfloat16 [1152, 1152], replicated, may hold values from -0.1875 to 0.1875
- log_scale: float32 [1], replicated, may hold values from 1 to 2.3
- bias: float32 [1], replicated, may hold values from -4 to -1
Outputs:
- img_grad: bfloat16 [131072, 1152], P('batch')
- txt_grad: bfloat16 [131072, 1152], P('batch')
- head_grad: float32 [1152, 1152], replicated
The draws below stay inside these ranges and needn't reach their ends.
All inputs are finite; a program needn't handle non-finite values.
Results may differ from the reference program's by a relative error of at most 0.0067.
Values may be sent and summed in bfloat16 or wider, within the bound.
A program may use at most 64 MiB of HBM per device.

```python
import jax
import jax.numpy as jnp
from jax import lax

E = 1152
ROWS = 512
TOKENS = 131072
N_BATCH = 256


def steps_of(stream_key, shape, shards, smallest, largest):
    factor_of, own = 1.0, jax.random.fold_in(stream_key, 6)
    for axis_at, shards_of in shards:
        draws = jnp.exp(jax.random.uniform(jax.random.fold_in(own, axis_at), (shards_of,), jnp.float32, smallest / len(shards), largest / len(shards)))
        factor_of = factor_of * jnp.repeat(draws, shape[axis_at] // shards_of).reshape([-1 if axis == axis_at else 1 for axis in range(len(shape))])
    return factor_of


def centred(own_key, extent, scale, reach, split=(), dtype=jnp.bfloat16):
    drawn = jax.random.normal(own_key, extent, jnp.float32) * scale
    if len(split) > 0:
        drawn = steps_of(own_key, extent, split, -0.22, 0.18) * drawn
    return jnp.clip(drawn, min=-reach, max=reach).astype(dtype)


def setup_inputs(seed: int = 0) -> dict:
    key_of = jax.random.split(jax.random.key(seed), 6)
    return {
        "img_emb": centred(key_of[0], (TOKENS, E), 0.03, 0.19921875, ((0, 256),)),
        "txt_feat": centred(key_of[1], (TOKENS, E), 0.03, 0.19921875, ((0, 256),)),
        "txt_head": centred(key_of[2], (E, E), E ** -0.5, 0.1875),
        "log_scale": jnp.clip(jax.random.uniform(key_of[3], (1,), jnp.float32, 1.0, 2.3), 1.0, 2.3),
        "bias": jnp.clip(jax.random.uniform(key_of[4], (1,), jnp.float32, -4.0, -1.0), -4.0, -1.0),
    }


def unit_rows(values):
    rinv = lax.rsqrt(lax.optimization_barrier(jnp.sum(values * values, axis=-1, keepdims=True)) + 1e-06)
    return (values * rinv, rinv)

def pair_weights(images, texts, scale, offset, own):
    logits = scale * jnp.dot(images, texts.T, preferred_element_type=jnp.float32) + offset
    count = images.shape[0]
    row_id = lax.broadcasted_iota(jnp.int32, (count, count), 0)
    col_id = lax.broadcasted_iota(jnp.int32, (count, count), 1)
    if own:
        sign = jnp.where(row_id == col_id, jnp.float32(1.0), jnp.float32(-1.0))
    else:
        sign = jnp.full((count, count), -1.0, jnp.float32)
    grads = sign * (jax.nn.sigmoid(sign * logits) - 1.0)
    return (scale * grads).astype(jnp.bfloat16)

def reference(img_emb, txt_feat, txt_head, log_scale, bias):
    scale = jnp.exp(log_scale[0])
    offset = bias[0]
    img_unit, img_rinv = unit_rows(img_emb.astype(jnp.float32))
    hidden = jnp.dot(txt_feat, txt_head, preferred_element_type=jnp.float32)
    txt_unit, txt_rinv = unit_rows(hidden)
    unit_img = img_unit.astype(jnp.bfloat16).reshape(N_BATCH, ROWS, E)
    unit_txt = txt_unit.astype(jnp.bfloat16).reshape(N_BATCH, ROWS, E)
    before = jnp.roll(unit_txt, 1, axis=0)
    after = jnp.roll(unit_txt, -1, axis=0)

    def one_block(blocks):
        images, own_txt, left_txt, right_txt = blocks
        weight_own = pair_weights(images, own_txt, scale, offset, True)
        weight_left = pair_weights(images, left_txt, scale, offset, False)
        weight_right = pair_weights(images, right_txt, scale, offset, False)
        unit_grad = jnp.dot(weight_own, own_txt, preferred_element_type=jnp.float32)
        unit_grad = unit_grad + jnp.dot(weight_left, left_txt, preferred_element_type=jnp.float32)
        unit_grad = unit_grad + jnp.dot(weight_right, right_txt, preferred_element_type=jnp.float32)
        part_own = jnp.dot(weight_own.T, images, preferred_element_type=jnp.float32)
        part_left = jnp.dot(weight_left.T, images, preferred_element_type=jnp.float32).astype(jnp.bfloat16)
        part_right = jnp.dot(weight_right.T, images, preferred_element_type=jnp.float32).astype(jnp.bfloat16)
        return (unit_grad, part_own, part_left, part_right)
    unit_grad, part_own, part_left, part_right = lax.map(one_block, (unit_img, unit_txt, before, after))
    text_unit_grad = part_own + jnp.roll(part_left, -1, axis=0).astype(jnp.float32)
    text_unit_grad = text_unit_grad + jnp.roll(part_right, 1, axis=0).astype(jnp.float32)
    unit_grad = unit_grad.reshape(N_BATCH * ROWS, E)
    text_unit_grad = text_unit_grad.reshape(N_BATCH * ROWS, E)
    img_grad = (unit_grad - img_unit * lax.optimization_barrier(jnp.sum(img_unit * unit_grad, axis=-1, keepdims=True))) * img_rinv
    hidden_grad = (text_unit_grad - txt_unit * lax.optimization_barrier(jnp.sum(txt_unit * text_unit_grad, axis=-1, keepdims=True))) * txt_rinv
    hidden_grad = hidden_grad.astype(jnp.bfloat16)
    txt_grad = jnp.dot(hidden_grad, txt_head.T, preferred_element_type=jnp.float32)
    head_grad = jnp.dot(txt_feat.T, hidden_grad, preferred_element_type=jnp.float32)
    return (img_grad.astype(jnp.bfloat16), txt_grad.astype(jnp.bfloat16), head_grad)
```

```python
import functools

import jax
import jax.numpy as jnp
from jax import lax
from jax.experimental import pallas as pl
from jax.experimental.pallas import tpu as pltpu
from jax.sharding import PartitionSpec as P

MESH = pl.DeviceIdType.MESH
F32 = jnp.float32
BF16 = jnp.bfloat16
ZS, XS, YS, CS = 8, 4, 4, 2
XY = XS * YS
E = 1152
ROWS = 512
HALF = E // 2
COLS = E // 128
UNITS = HALF // 16
PA = 14
PB = 13
NA = PA * XY
NB = PB * ZS
NT = NA + NB


def coords(me):
    return (me // (XS * YS * CS), (me // (YS * CS)) % XS, (me // CS) % YS, me % CS)


def device(z, x, y, c):
    return ((z * XS + x) * YS + y) * CS + c


def xy_member(me, d):
    z, x, y, c = coords(me)
    x = (x + d // YS) % XS
    y = (y + d % YS) % YS
    return (device(z, x, y, c), x * YS + y)


def xy_source(me, d):
    z, x, y, c = coords(me)
    return ((x + XS - d // YS) % XS) * YS + (y + YS - d % YS) % YS


def z_member(me, d):
    z, x, y, c = coords(me)
    z = (z + d) % ZS
    return (device(z, x, y, c), z)


def other_core(me):
    return me + 1 - 2 * (me % CS)


def remote(src, dst, ssem, rsem, to):
    return pltpu.make_async_remote_copy(
        src_ref=src, dst_ref=dst, send_sem=ssem, recv_sem=rsem,
        device_id=(to,), device_id_type=MESH,
    )


def each(lo, hi, body):
    def step(i, carry):
        body(i)
        return carry

    lax.fori_loop(lo, hi, step, 0)


def all_reduce(me, w, out, s):
    z, x, y, c = coords(me)
    p = x * YS + y
    nbr = other_core(me)

    def a1(d):
        to, q = xy_member(me, d)
        return remote(w.at[pl.ds(q * PA, PA)], s.ra1.at[d], s.s1.at[d], s.r1.at[d], to)

    def b1(d):
        to, q = z_member(me, d)
        return remote(w.at[pl.ds(NA + q * PB, PB)], s.rb1.at[d], s.s1.at[XY + d], s.r1.at[XY + d], to)

    def a2(d):
        to, q = z_member(me, d)
        return remote(s.sa.at[pl.ds(q * 2, 2)], s.ra2.at[d], s.s2.at[XY + d], s.r2.at[XY + d], to)

    def b2(d):
        to, q = xy_member(me, d)
        return remote(s.sb.at[pl.ds(q, 1)], s.rb2.at[d], s.s2.at[d], s.r2.at[d], to)

    def a3(d):
        to, q = z_member(me, d)
        here = s.ga.at[pl.ds(z * 2, 2)]
        return remote(here, here, s.s3.at[XY + d], s.r3.at[XY + d], to)

    def b3(d):
        to, q = xy_member(me, d)
        here = s.gb.at[pl.ds(p, 1)]
        return remote(here, here, s.s3.at[d], s.r3.at[d], to)

    def a4(d):
        to, q = xy_member(me, d)
        return remote(s.ga.at[pl.ds(0, PA)], out.at[c, pl.ds(p * PA, PA)], s.s4.at[d], s.r4.at[d], to)

    def b4(d):
        to, q = z_member(me, d)
        return remote(s.gb.at[pl.ds(0, PB)], out.at[c, pl.ds(NA + z * PB, PB)], s.s4.at[XY + d], s.r4.at[XY + d], to)

    def fa(d):
        q = xy_source(me, d)
        here = out.at[c, pl.ds(q * PA, PA)]
        return remote(here, here, s.s5.at[d], s.r5.at[d], nbr)

    def fb(d):
        q = z_member(me, ZS - d)[1]
        here = out.at[c, pl.ds(NA + q * PB, PB)]
        return remote(here, here, s.s5.at[XY + d], s.r5.at[XY + d], nbr)

    each(1, ZS, lambda d: b1(d).start())
    each(1, XY, lambda d: a1(d).start())
    each(1, ZS, lambda d: b1(d).wait_recv())

    def sum_b1(i):
        total = w[NA + z * PB + i].astype(F32) + jnp.sum(s.rb1[1:, i].astype(F32), axis=0)
        s.sb[i] = total.astype(BF16)

    each(0, PB, sum_b1)
    s.sb[PB:] = jnp.zeros((XY - PB, 16, 128), BF16)
    each(1, XY, lambda d: b2(d).start())
    each(1, XY, lambda d: a1(d).wait_recv())

    def sum_a1(i):
        total = w[p * PA + i].astype(F32) + jnp.sum(s.ra1[1:, i].astype(F32), axis=0)
        s.sa[i] = total.astype(BF16)

    each(0, PA, sum_a1)
    s.sa[PA:] = jnp.zeros((2 * ZS - PA, 16, 128), BF16)
    each(1, ZS, lambda d: a2(d).start())
    each(1, XY, lambda d: b2(d).wait_recv())
    total = s.sb[p].astype(F32) + jnp.sum(s.rb2[1:, 0].astype(F32), axis=0)
    s.gb[p] = total.astype(BF16)
    each(1, XY, lambda d: b3(d).start())
    each(1, ZS, lambda d: a2(d).wait_recv())

    def sum_a2(i):
        total = s.sa[z * 2 + i].astype(F32) + jnp.sum(s.ra2[1:, i].astype(F32), axis=0)
        s.ga[z * 2 + i] = total.astype(BF16)

    each(0, 2, sum_a2)
    each(1, ZS, lambda d: a3(d).start())
    each(1, XY, lambda d: b3(d).wait_recv())
    each(1, ZS, lambda d: b4(d).start())
    own_b = pltpu.make_async_copy(s.gb.at[pl.ds(0, PB)], out.at[c, pl.ds(NA + z * PB, PB)], s.own.at[0])
    own_b.start()
    each(1, ZS, lambda d: a3(d).wait_recv())
    each(1, XY, lambda d: a4(d).start())
    own_a = pltpu.make_async_copy(s.ga.at[pl.ds(0, PA)], out.at[c, pl.ds(p * PA, PA)], s.own.at[1])
    own_a.start()
    own_b.wait()
    own_a.wait()
    fb(0).start()
    fa(0).start()

    def pass_b(d):
        b4(d).wait_recv()
        fb(d).start()

    def pass_a(d):
        a4(d).wait_recv()
        fa(d).start()

    each(1, ZS, pass_b)
    each(1, XY, pass_a)
    for first, last in ((a1, b1), (b2, a2), (b3, a3), (a4, b4)):
        each(1, XY, lambda d: first(d).wait_send())
        each(1, ZS, lambda d: last(d).wait_send())
    each(0, XY, lambda d: fa(d).wait())
    each(0, ZS, lambda d: fb(d).wait())


class Names:
    pass


AR_SCRATCH = dict(
    ra1=pltpu.VMEM((XY, PA, 16, 128), BF16),
    rb1=pltpu.VMEM((ZS, PB, 16, 128), BF16),
    sa=pltpu.VMEM((2 * ZS, 16, 128), BF16),
    sb=pltpu.VMEM((XY, 16, 128), BF16),
    ra2=pltpu.VMEM((ZS, 2, 16, 128), BF16),
    rb2=pltpu.VMEM((XY, 1, 16, 128), BF16),
    ga=pltpu.VMEM((2 * ZS, 16, 128), BF16),
    gb=pltpu.VMEM((XY, 16, 128), BF16),
    s1=pltpu.SemaphoreType.DMA((XY + ZS,)),
    r1=pltpu.SemaphoreType.DMA((XY + ZS,)),
    s2=pltpu.SemaphoreType.DMA((XY + ZS,)),
    r2=pltpu.SemaphoreType.DMA((XY + ZS,)),
    s3=pltpu.SemaphoreType.DMA((XY + ZS,)),
    r3=pltpu.SemaphoreType.DMA((XY + ZS,)),
    s4=pltpu.SemaphoreType.DMA((XY + ZS,)),
    r4=pltpu.SemaphoreType.DMA((XY + ZS,)),
    s5=pltpu.SemaphoreType.DMA((XY + ZS,)),
    r5=pltpu.SemaphoreType.DMA((XY + ZS,)),
    own=pltpu.SemaphoreType.DMA((2,)),
)


def enter(me):
    barrier = pltpu.get_barrier_semaphore()

    def greet(to):
        pl.semaphore_signal(barrier, inc=1, device_id=(to,), device_id_type=MESH)

    greet(other_core(me))
    each(1, XY, lambda d: greet(xy_member(me, d)[0]))
    each(1, ZS, lambda d: greet(z_member(me, d)[0]))
    pl.semaphore_wait(barrier, XY + ZS - 1)


def head_kernel(txt_ref, hid_ref, out, *scratch):
    me = lax.axis_index("batch")
    c = me % CS
    s = Names()
    for name, ref in zip(list(HEAD_SCRATCH), scratch):
        setattr(s, name, ref)
    enter(me)
    nbr = other_core(me)
    theirs = pl.ds(pl.multiple_of((1 - c) * HALF, HALF), HALF)
    hid_copy = remote(hid_ref, s.hid_nbr, s.cs.at[1], s.cr.at[1], nbr)
    hid_copy.start()

    def flip(i):
        cols = pl.ds(pl.multiple_of(i * 128, 128), 128)
        s.txt_t[cols, :] = txt_ref[:, cols].T

    each(0, COLS, flip)
    txt_copy = remote(s.txt_t.at[theirs], s.txt_nbr, s.cs.at[0], s.cr.at[0], nbr)
    txt_copy.start()
    txt_copy.wait_recv()
    hid_copy.wait_recv()
    step = 6

    def rows_of(i):
        at = pl.multiple_of(i * 16 * step, 16 * step)
        mine = s.txt_t[pl.ds(pl.multiple_of(c * HALF + at, 16 * step), 16 * step), :]
        value = jnp.dot(mine, hid_ref[...], preferred_element_type=F32)
        value += jnp.dot(s.txt_nbr[pl.ds(at, 16 * step), :], s.hid_nbr[...], preferred_element_type=F32)
        value = value.astype(BF16)
        for r in range(step):
            for col in range(COLS):
                s.w[(i * step + r) * COLS + col] = value[r * 16:(r + 1) * 16, col * 128:(col + 1) * 128]

    each(0, UNITS // step, rows_of)
    s.w[UNITS * COLS:] = jnp.zeros((NT - UNITS * COLS, 16, 128), BF16)
    all_reduce(me, s.w, out, s)
    txt_copy.wait_send()
    hid_copy.wait_send()


HEAD_SCRATCH = dict(
    w=pltpu.VMEM((NT, 16, 128), BF16),
    txt_t=pltpu.VMEM((E, ROWS), BF16),
    txt_nbr=pltpu.VMEM((HALF, ROWS), BF16),
    hid_nbr=pltpu.VMEM((ROWS, E), BF16),
    cs=pltpu.SemaphoreType.DMA((2,)),
    cr=pltpu.SemaphoreType.DMA((2,)),
    **AR_SCRATCH,
)


def head_tiles(txt_feat, hidden_grad):
    return pl.pallas_call(
        head_kernel,
        out_shape=jax.ShapeDtypeStruct((CS, NT, 16, 128), BF16),
        in_specs=[pl.BlockSpec(memory_space=pltpu.VMEM)] * 2,
        out_specs=pl.BlockSpec(memory_space=pl.ANY),
        scratch_shapes=list(HEAD_SCRATCH.values()),
        compiler_params=pltpu.CompilerParams(
            collective_id=0, has_side_effects=True, vmem_limit_bytes=48 << 20
        ),
        name="head",
    )(txt_feat, hidden_grad)


def lay_kernel(step, tiles_ref, out_ref):
    for r in range(step):
        for col in range(COLS):
            out_ref[r * 16:(r + 1) * 16, col * 128:(col + 1) * 128] = tiles_ref[r * COLS + col].astype(F32)


def lay_out(tiles):
    step = 6
    blocks = UNITS // step
    return pl.pallas_call(
        functools.partial(lay_kernel, step),
        out_shape=jax.ShapeDtypeStruct((E, E), F32),
        grid=(CS * blocks,),
        in_specs=[pl.BlockSpec((None, step * COLS, 16, 128), lambda i: (i // blocks, i % blocks, 0, 0))],
        out_specs=pl.BlockSpec((step * 16, E), lambda i: (i, 0)),
        name="lay_out",
    )(tiles)


def passed_along(block, axis, distance):
    devices = range(lax.axis_size(axis))
    route = [((i - distance) % len(devices), i) for i in devices]
    return lax.ppermute(block, axis, route)


def unit_rows(values):
    rinv = lax.rsqrt(jnp.sum(values * values, axis=-1, keepdims=True) + 1e-06)
    return (values * rinv, rinv)


def pair_weights(images, texts, scale, offset, diag_at):
    logits = (
        scale
        * lax.dot_general(
            images, texts, (((1,), (1,)), ((), ())), preferred_element_type=jnp.float32
        )
        + offset
    )
    shape = (images.shape[0], texts.shape[0])
    row_id = lax.broadcasted_iota(jnp.int32, shape, 0)
    col_id = lax.broadcasted_iota(jnp.int32, shape, 1)
    sign = jnp.where(col_id == row_id + diag_at, jnp.float32(1.0), jnp.float32(-1.0))
    grads = sign * (jax.nn.sigmoid(sign * logits) - 1.0)
    return (scale * grads).astype(jnp.bfloat16)


def image_terms(weight, images):
    return lax.dot_general(
        weight, images, (((0,), (0,)), ((), ())), preferred_element_type=jnp.float32
    )


def fetch_left(unit_txt):
    return passed_along(unit_txt, "batch", 1)


def return_left(part):
    return passed_along(part, "batch", -1)


def return_right(part):
    return passed_along(part, "batch", 1)


def shards(img_emb, txt_feat, txt_head, log_scale, bias):
    rows = img_emb.shape[0]
    scale = jnp.exp(log_scale[0])
    offset = bias[0]
    img_unit, img_rinv = unit_rows(img_emb.astype(jnp.float32))
    hidden = jnp.dot(txt_feat, txt_head, preferred_element_type=jnp.float32)
    txt_unit, txt_rinv = unit_rows(hidden)
    unit_img = img_unit.astype(jnp.bfloat16)
    unit_txt = txt_unit.astype(jnp.bfloat16)
    weight_own = pair_weights(unit_img, unit_txt, scale, offset, 0)
    unit_grad = jnp.dot(weight_own, unit_txt, preferred_element_type=jnp.float32)
    part_own = image_terms(weight_own, unit_img)
    left_txt = fetch_left(unit_txt)
    weight_left = pair_weights(unit_img, left_txt, scale, offset, rows)
    unit_grad = unit_grad + jnp.dot(weight_left, left_txt, preferred_element_type=jnp.float32)
    part_left = image_terms(weight_left, unit_img).astype(jnp.bfloat16)
    back_left = return_left(part_left)
    right_txt = passed_along(unit_txt, "batch", -1)
    weight_right = pair_weights(unit_img, right_txt, scale, offset, rows)
    unit_grad = unit_grad + jnp.dot(weight_right, right_txt, preferred_element_type=jnp.float32)
    back_right = return_right(image_terms(weight_right, unit_img).astype(jnp.bfloat16))
    text_unit_grad = part_own + back_left.astype(jnp.float32) + back_right.astype(jnp.float32)
    img_grad = (
        unit_grad - img_unit * jnp.sum(img_unit * unit_grad, axis=-1, keepdims=True)
    ) * img_rinv
    hidden_grad = (
        text_unit_grad - txt_unit * jnp.sum(txt_unit * text_unit_grad, axis=-1, keepdims=True)
    ) * txt_rinv
    hidden_grad = hidden_grad.astype(jnp.bfloat16)
    txt_grad = lax.dot_general(
        hidden_grad, txt_head, (((1,), (1,)), ((), ())), preferred_element_type=jnp.float32
    )
    head_grad = lay_out(head_tiles(txt_feat, hidden_grad))
    return (img_grad.astype(jnp.bfloat16), txt_grad.astype(jnp.bfloat16), head_grad)


def solution(mesh):
    return jax.shard_map(
        shards,
        mesh=mesh,
        in_specs=(P("batch", None), P("batch", None), P(), P(), P()),
        out_specs=(P("batch", None), P("batch", None), P()),
        check_vma=False,
    )
```

```python
import functools

import jax
import jax.numpy as jnp
from jax import lax
from jax.experimental import pallas as pl
from jax.experimental.pallas import tpu as pltpu
from jax.sharding import PartitionSpec as P

MESH = pl.DeviceIdType.MESH
F32 = jnp.float32
BF16 = jnp.bfloat16
ZS, XS, YS, CS = 8, 4, 4, 2
XY = XS * YS
E = 1152
ROWS = 512
HALF = E // 2
COLS = E // 128
UNITS = HALF // 16
PA = 14
PB = 13
NA = PA * XY
NB = PB * ZS
NT = NA + NB


def coords(me):
    return (me // (XS * YS * CS), (me // (YS * CS)) % XS, (me // CS) % YS, me % CS)


def device(z, x, y, c):
    return ((z * XS + x) * YS + y) * CS + c


def xy_member(me, d):
    z, x, y, c = coords(me)
    x = (x + d // YS) % XS
    y = (y + d % YS) % YS
    return (device(z, x, y, c), x * YS + y)


def xy_source(me, d):
    z, x, y, c = coords(me)
    return ((x + XS - d // YS) % XS) * YS + (y + YS - d % YS) % YS


def z_member(me, d):
    z, x, y, c = coords(me)
    z = (z + d) % ZS
    return (device(z, x, y, c), z)


def other_core(me):
    return me + 1 - 2 * (me % CS)


def remote(src, dst, ssem, rsem, to):
    return pltpu.make_async_remote_copy(
        src_ref=src, dst_ref=dst, send_sem=ssem, recv_sem=rsem,
        device_id=(to,), device_id_type=MESH,
    )


def each(lo, hi, body):
    def step(i, carry):
        body(i)
        return carry

    lax.fori_loop(lo, hi, step, 0)


def all_reduce(me, w, out, s, after_first, after_second, after_last):
    z, x, y, c = coords(me)
    p = x * YS + y
    nbr = other_core(me)

    def a1(d):
        to, q = xy_member(me, d)
        return remote(w.at[pl.ds(q * PA, PA)], s.ra1.at[d], s.s1.at[d], s.r1.at[d], to)

    def b1(d):
        to, q = z_member(me, d)
        return remote(w.at[pl.ds(NA + q * PB, PB)], s.rb1.at[d], s.s1.at[XY + d], s.r1.at[XY + d], to)

    def a2(d):
        to, q = z_member(me, d)
        return remote(s.sa.at[pl.ds(q * 2, 2)], s.ra2.at[d], s.s2.at[XY + d], s.r2.at[XY + d], to)

    def b2(d):
        to, q = xy_member(me, d)
        return remote(s.sb.at[pl.ds(q, 1)], s.rb2.at[d], s.s2.at[d], s.r2.at[d], to)

    def a3(d):
        to, q = z_member(me, d)
        here = s.ga.at[pl.ds(z * 2, 2)]
        return remote(here, here, s.s3.at[XY + d], s.r3.at[XY + d], to)

    def b3(d):
        to, q = xy_member(me, d)
        here = s.gb.at[pl.ds(p, 1)]
        return remote(here, here, s.s3.at[d], s.r3.at[d], to)

    def a4(d):
        to, q = xy_member(me, d)
        return remote(s.ga.at[pl.ds(0, PA)], out.at[c, pl.ds(p * PA, PA)], s.s4.at[d], s.r4.at[d], to)

    def b4(d):
        to, q = z_member(me, d)
        return remote(s.gb.at[pl.ds(0, PB)], out.at[c, pl.ds(NA + z * PB, PB)], s.s4.at[XY + d], s.r4.at[XY + d], to)

    def fa(d):
        q = xy_source(me, d)
        here = out.at[c, pl.ds(q * PA, PA)]
        return remote(here, here, s.s5.at[d], s.r5.at[d], nbr)

    def fb(d):
        q = z_member(me, ZS - d)[1]
        here = out.at[c, pl.ds(NA + q * PB, PB)]
        return remote(here, here, s.s5.at[XY + d], s.r5.at[XY + d], nbr)

    each(1, ZS, lambda d: b1(d).start())
    each(1, XY, lambda d: a1(d).start())
    after_first()
    each(1, ZS, lambda d: b1(d).wait_recv())

    def sum_b1(i):
        total = w[NA + z * PB + i].astype(F32) + jnp.sum(s.rb1[1:, i].astype(F32), axis=0)
        s.sb[i] = total.astype(BF16)

    each(0, PB, sum_b1)
    s.sb[PB:] = jnp.zeros((XY - PB, 16, 128), BF16)
    each(1, XY, lambda d: b2(d).start())
    each(1, XY, lambda d: a1(d).wait_recv())

    def sum_a1(i):
        total = w[p * PA + i].astype(F32) + jnp.sum(s.ra1[1:, i].astype(F32), axis=0)
        s.sa[i] = total.astype(BF16)

    each(0, PA, sum_a1)
    s.sa[PA:] = jnp.zeros((2 * ZS - PA, 16, 128), BF16)
    each(1, ZS, lambda d: a2(d).start())
    after_second()
    each(1, XY, lambda d: b2(d).wait_recv())
    total = s.sb[p].astype(F32) + jnp.sum(s.rb2[1:, 0].astype(F32), axis=0)
    s.gb[p] = total.astype(BF16)
    each(1, XY, lambda d: b3(d).start())
    each(1, ZS, lambda d: a2(d).wait_recv())

    def sum_a2(i):
        total = s.sa[z * 2 + i].astype(F32) + jnp.sum(s.ra2[1:, i].astype(F32), axis=0)
        s.ga[z * 2 + i] = total.astype(BF16)

    each(0, 2, sum_a2)
    each(1, ZS, lambda d: a3(d).start())
    each(1, XY, lambda d: b3(d).wait_recv())
    each(1, ZS, lambda d: b4(d).start())
    own_b = pltpu.make_async_copy(s.gb.at[pl.ds(0, PB)], out.at[c, pl.ds(NA + z * PB, PB)], s.own.at[0])
    own_b.start()
    each(1, ZS, lambda d: a3(d).wait_recv())
    each(1, XY, lambda d: a4(d).start())
    own_a = pltpu.make_async_copy(s.ga.at[pl.ds(0, PA)], out.at[c, pl.ds(p * PA, PA)], s.own.at[1])
    own_a.start()
    own_b.wait()
    own_a.wait()
    fb(0).start()
    fa(0).start()
    after_last()

    def pass_b(d):
        b4(d).wait_recv()
        fb(d).start()

    def pass_a(d):
        a4(d).wait_recv()
        fa(d).start()

    each(1, ZS, pass_b)
    each(1, XY, pass_a)
    for first, last in ((a1, b1), (b2, a2), (b3, a3), (a4, b4)):
        each(1, XY, lambda d: first(d).wait_send())
        each(1, ZS, lambda d: last(d).wait_send())
    each(0, XY, lambda d: fa(d).wait())
    each(0, ZS, lambda d: fb(d).wait())


class Names:
    pass


AR_SCRATCH = dict(
    ra1=pltpu.VMEM((XY, PA, 16, 128), BF16),
    rb1=pltpu.VMEM((ZS, PB, 16, 128), BF16),
    sa=pltpu.VMEM((2 * ZS, 16, 128), BF16),
    sb=pltpu.VMEM((XY, 16, 128), BF16),
    ra2=pltpu.VMEM((ZS, 2, 16, 128), BF16),
    rb2=pltpu.VMEM((XY, 1, 16, 128), BF16),
    ga=pltpu.VMEM((2 * ZS, 16, 128), BF16),
    gb=pltpu.VMEM((XY, 16, 128), BF16),
    s1=pltpu.SemaphoreType.DMA((XY + ZS,)),
    r1=pltpu.SemaphoreType.DMA((XY + ZS,)),
    s2=pltpu.SemaphoreType.DMA((XY + ZS,)),
    r2=pltpu.SemaphoreType.DMA((XY + ZS,)),
    s3=pltpu.SemaphoreType.DMA((XY + ZS,)),
    r3=pltpu.SemaphoreType.DMA((XY + ZS,)),
    s4=pltpu.SemaphoreType.DMA((XY + ZS,)),
    r4=pltpu.SemaphoreType.DMA((XY + ZS,)),
    s5=pltpu.SemaphoreType.DMA((XY + ZS,)),
    r5=pltpu.SemaphoreType.DMA((XY + ZS,)),
    own=pltpu.SemaphoreType.DMA((2,)),
)


def greet_all(me):
    barrier = pltpu.get_barrier_semaphore()

    def greet(to):
        pl.semaphore_signal(barrier, inc=1, device_id=(to,), device_id_type=MESH)

    greet(far_device(me))
    greet(other_core(me))
    each(1, XY, lambda d: greet(xy_member(me, d)[0]))
    each(1, ZS, lambda d: greet(z_member(me, d)[0]))
    return barrier


RC = 128
FAR = 256


def far_device(me):
    ring = ZS * XS * YS * CS
    return lax.rem(me + ring - 1 + 2 * (me % CS), ring)


def rows_at(start, size):
    return pl.ds(pl.multiple_of(start, size), size)


def dot_nt(a, b):
    return lax.dot_general(a, b, (((1,), (1,)), ((), ())), preferred_element_type=F32)


def dot_nn(a, b):
    return jnp.dot(a, b, preferred_element_type=F32)


def unit_of(values):
    rinv = lax.rsqrt(jnp.sum(values * values, axis=-1, keepdims=True) + 1e-06)
    return (values * rinv, rinv)


def own_diagonal(shape, start):
    row = lax.broadcasted_iota(jnp.int32, shape, 0) + start
    return lax.broadcasted_iota(jnp.int32, shape, 1) == row


def main_kernel(img_hbm, feat_hbm, head_hbm, scale_ref, bias_ref, tiles, txt_out, img_out, *scratch):
    me = lax.axis_index("batch")
    c = me % CS
    near = other_core(me)
    far = far_device(me)
    s = Names()
    for name, ref in zip(list(MAIN_SCRATCH), scratch):
        setattr(s, name, ref)
    img_in = pltpu.make_async_copy(img_hbm, s.img, s.ins.at[0])
    feat_in = pltpu.make_async_copy(feat_hbm, s.feat, s.ins.at[1])
    head_in = pltpu.make_async_copy(head_hbm, s.head, s.ins.at[2])
    img_in.start()
    feat_in.start()
    head_in.start()
    barrier = greet_all(me)
    half = 0.5 * jnp.exp(jnp.full((1, 1), scale_ref[0], F32))
    shift = 0.5 * jnp.full((1, 1), bias_ref[0], F32)

    def weights(dots):
        return jnp.tanh(dots * half + shift) * half + half

    def img_far(k):
        return remote(s.imgs.at[pl.ds(k * FAR, FAR)], s.imgs.at[pl.ds(2 * ROWS + k * FAR, FAR)],
                      s.es.at[k], s.er.at[k], far)

    def txt_far(k):
        return remote(s.txts.at[pl.ds(k * FAR, FAR)], s.txts.at[pl.ds(2 * ROWS + k * FAR, FAR)],
                      s.es.at[2 + k], s.er.at[2 + k], far)

    img_near = remote(s.imgs.at[pl.ds(0, ROWS)], s.imgs.at[pl.ds(ROWS, ROWS)], s.es.at[4], s.er.at[4], near)
    txt_near = remote(s.txts.at[pl.ds(0, ROWS)], s.txts.at[pl.ds(ROWS, ROWS)], s.es.at[5], s.er.at[5], near)
    theirs = rows_at((1 - c) * HALF, HALF)
    feat_near = remote(s.feat_t.at[theirs], s.feat_nbr, s.es.at[6], s.er.at[6], near)

    def hid_near(j):
        return remote(s.hid.at[rows_at(j * RC, RC)], s.hid.at[rows_at(ROWS + j * RC, RC)],
                      s.hs.at[j], s.hr.at[j], near)

    img_in.wait()

    def unit_images(j):
        at = rows_at(j * RC, RC)
        unit, rinv = unit_of(s.img[at, :].astype(F32))
        s.imgs[at, :] = unit.astype(BF16)
        s.img_rinv[at, :] = rinv

    each(0, FAR // RC, unit_images)
    pl.semaphore_wait(barrier, XY + ZS)
    img_far(0).start()
    each(FAR // RC, ROWS // RC, unit_images)
    img_far(1).start()
    img_near.start()
    feat_in.wait()
    head_in.wait()

    def unit_texts(j):
        at = rows_at(j * RC, RC)
        unit, rinv = unit_of(dot_nn(s.feat[at, :], s.head[...]))
        s.txt_unit[at, :] = unit
        s.txts[at, :] = unit.astype(BF16)
        s.txt_rinv[at, :] = rinv

    each(0, ROWS // RC, unit_texts)
    txt_near.start()

    def flip(i):
        cols = rows_at(i * 128, 128)
        s.feat_t[cols, :] = s.feat[:, cols].T

    each(0, COLS, flip)
    feat_near.start()
    img_near.wait_recv()

    def text_first(j):
        at = rows_at(j * RC, RC)
        images = s.imgs[0:2 * ROWS, :]
        weight = weights(dot_nt(s.txts[at, :], images))
        weight = weight - jnp.where(own_diagonal(weight.shape, j * RC), 2.0 * half, 0.0)
        s.text_sum[at, :] = dot_nn(weight.astype(BF16), images)

    each(0, ROWS // RC, text_first)
    img_far(0).wait_recv()

    def text_second(j):
        at = rows_at(j * RC, RC)
        images = s.imgs[2 * ROWS:2 * ROWS + FAR, :]
        weight = weights(dot_nt(s.txts[at, :], images)).astype(BF16)
        s.text_sum[at, :] += dot_nn(weight, images)

    each(0, ROWS // RC, text_second)
    img_far(1).wait_recv()

    def text_third(j):
        at = rows_at(j * RC, RC)
        images = s.imgs[2 * ROWS + FAR:3 * ROWS, :]
        weight = weights(dot_nt(s.txts[at, :], images)).astype(BF16)
        total = s.text_sum[at, :] + dot_nn(weight, images)
        unit = s.txt_unit[at, :]
        along = jnp.sum(unit * total, axis=-1, keepdims=True)
        s.hid[at, :] = ((total - unit * along) * s.txt_rinv[at, :]).astype(BF16)
        hid_near(j).start()

    each(0, ROWS // RC, text_third)
    step = 6
    block = 16 * step

    def head_own(i):
        mine = s.feat_t[rows_at(c * HALF + i * block, block), :]
        s.head_sum[rows_at(i * block, block), :] = dot_nn(mine, s.hid[0:ROWS, :])

    each(0, UNITS // step, head_own)
    feat_near.wait_recv()
    each(0, ROWS // RC, lambda j: hid_near(j).wait_recv())

    def head_near(i):
        at = rows_at(i * block, block)
        value = s.head_sum[at, :] + dot_nn(s.feat_nbr[at, :], s.hid[ROWS:2 * ROWS, :])
        value = value.astype(BF16)
        for r in range(step):
            for col in range(COLS):
                s.w[(i * step + r) * COLS + col] = value[r * 16:(r + 1) * 16, col * 128:(col + 1) * 128]

    each(0, UNITS // step, head_near)
    s.w[UNITS * COLS:] = jnp.zeros((NT - UNITS * COLS, 16, 128), BF16)

    txt_write = pltpu.make_async_copy(s.txt_grad, txt_out, s.outs.at[0])
    img_write = pltpu.make_async_copy(s.img_grad, img_out, s.outs.at[1])

    def after_first():
        def text_grads(j):
            at = rows_at(j * RC, RC)
            s.txt_grad[at, :] = dot_nt(s.hid[at, :], s.head[...]).astype(BF16)

        each(0, ROWS // RC, text_grads)
        txt_write.start()
        txt_near.wait_recv()

        def image_first(j):
            at = rows_at(j * RC, RC)
            texts = s.txts[0:2 * ROWS, :]
            weight = weights(dot_nt(s.imgs[at, :], texts))
            weight = weight - jnp.where(own_diagonal(weight.shape, j * RC), 2.0 * half, 0.0)
            s.img_sum[at, :] = dot_nn(weight.astype(BF16), texts)

        each(0, ROWS // RC, image_first)

    def after_second():
        txt_far(0).start()
        txt_far(1).start()

    def after_last():
        txt_far(0).wait_recv()
        txt_far(1).wait_recv()

        def image_second(j):
            at = rows_at(j * RC, RC)
            texts = s.txts[2 * ROWS:3 * ROWS, :]
            weight = weights(dot_nt(s.imgs[at, :], texts)).astype(BF16)
            total = s.img_sum[at, :] + dot_nn(weight, texts)
            rinv = s.img_rinv[at, :]
            unit = s.img[at, :].astype(F32) * rinv
            along = jnp.sum(unit * total, axis=-1, keepdims=True)
            s.img_grad[at, :] = ((total - unit * along) * rinv).astype(BF16)

        each(0, ROWS // RC, image_second)
        img_write.start()

    all_reduce(me, s.w, tiles, s, after_first, after_second, after_last)
    for k in range(2):
        img_far(k).wait_send()
        txt_far(k).wait_send()
    img_near.wait_send()
    txt_near.wait_send()
    feat_near.wait_send()
    each(0, ROWS // RC, lambda j: hid_near(j).wait_send())
    txt_write.wait()
    img_write.wait()


MAIN_SCRATCH = dict(
    img=pltpu.VMEM((ROWS, E), BF16),
    feat=pltpu.VMEM((ROWS, E), BF16),
    head=pltpu.VMEM((E, E), BF16),
    imgs=pltpu.VMEM((3 * ROWS, E), BF16),
    txts=pltpu.VMEM((3 * ROWS, E), BF16),
    img_rinv=pltpu.VMEM((ROWS, 1), F32),
    txt_rinv=pltpu.VMEM((ROWS, 1), F32),
    txt_unit=pltpu.VMEM((ROWS, E), F32),
    text_sum=pltpu.VMEM((ROWS, E), F32),
    img_sum=pltpu.VMEM((ROWS, E), F32),
    hid=pltpu.VMEM((2 * ROWS, E), BF16),
    feat_t=pltpu.VMEM((E, ROWS), BF16),
    feat_nbr=pltpu.VMEM((HALF, ROWS), BF16),
    head_sum=pltpu.VMEM((HALF, E), F32),
    w=pltpu.VMEM((NT, 16, 128), BF16),
    txt_grad=pltpu.VMEM((ROWS, E), BF16),
    img_grad=pltpu.VMEM((ROWS, E), BF16),
    ins=pltpu.SemaphoreType.DMA((3,)),
    outs=pltpu.SemaphoreType.DMA((2,)),
    es=pltpu.SemaphoreType.DMA((7,)),
    er=pltpu.SemaphoreType.DMA((7,)),
    hs=pltpu.SemaphoreType.DMA((4,)),
    hr=pltpu.SemaphoreType.DMA((4,)),
    **AR_SCRATCH,
)


def main_call(img_emb, txt_feat, txt_head, log_scale, bias):
    return pl.pallas_call(
        main_kernel,
        out_shape=(
            jax.ShapeDtypeStruct((CS, NT, 16, 128), BF16),
            jax.ShapeDtypeStruct((ROWS, E), BF16),
            jax.ShapeDtypeStruct((ROWS, E), BF16),
        ),
        in_specs=[pl.BlockSpec(memory_space=pl.ANY)] * 3 + [pl.BlockSpec(memory_space=pltpu.SMEM)] * 2,
        out_specs=[pl.BlockSpec(memory_space=pl.ANY)] * 3,
        scratch_shapes=list(MAIN_SCRATCH.values()),
        compiler_params=pltpu.CompilerParams(
            collective_id=0, has_side_effects=True, vmem_limit_bytes=56 << 20
        ),
        name="main",
    )(img_emb, txt_feat, txt_head, log_scale, bias)


LAY = 96


def final_kernel(tiles_hbm, txt_hbm, img_hbm, head_out, txt_out, img_out, tiles, head, txt, img, sems):
    txt_in = pltpu.make_async_copy(txt_hbm, txt, sems.at[0])
    img_in = pltpu.make_async_copy(img_hbm, img, sems.at[1])
    txt_back = pltpu.make_async_copy(txt, txt_out, sems.at[2])
    img_back = pltpu.make_async_copy(img, img_out, sems.at[3])
    per = LAY // 16 * COLS
    blocks = HALF // LAY

    def read(i):
        at = pl.ds((i % blocks) * per, per)
        return pltpu.make_async_copy(tiles_hbm.at[i // blocks, at], tiles.at[i // blocks, at], sems.at[4 + i])

    def write(i):
        at = rows_at(i * LAY, LAY)
        return pltpu.make_async_copy(head.at[at], head_out.at[at], sems.at[4 + CS * blocks + i])

    each(0, CS * blocks, lambda i: read(i).start())
    txt_in.start()
    img_in.start()

    def lay(i):
        read(i).wait()
        for r in range(LAY // 16):
            for col in range(COLS):
                value = tiles[i // blocks, (i % blocks) * per + r * COLS + col]
                head[pl.ds(pl.multiple_of(i * LAY + r * 16, 16), 16), col * 128:(col + 1) * 128] = value.astype(F32)
        write(i).start()

    each(0, CS * blocks, lay)
    txt_in.wait()
    txt_back.start()
    img_in.wait()
    img_back.start()
    each(0, CS * blocks, lambda i: write(i).wait())
    txt_back.wait()
    img_back.wait()


def final_call(tiles, txt_grad, img_grad):
    return pl.pallas_call(
        final_kernel,
        out_shape=(
            jax.ShapeDtypeStruct((E, E), F32),
            jax.ShapeDtypeStruct((ROWS, E), BF16),
            jax.ShapeDtypeStruct((ROWS, E), BF16),
        ),
        in_specs=[pl.BlockSpec(memory_space=pl.ANY)] * 3,
        out_specs=[pl.BlockSpec(memory_space=pl.ANY)] * 3,
        scratch_shapes=[
            pltpu.VMEM((CS, NT, 16, 128), BF16),
            pltpu.VMEM((E, E), F32),
            pltpu.VMEM((ROWS, E), BF16),
            pltpu.VMEM((ROWS, E), BF16),
            pltpu.SemaphoreType.DMA((4 + 2 * CS * HALF // LAY,)),
        ],
        compiler_params=pltpu.CompilerParams(vmem_limit_bytes=56 << 20),
        name="final",
    )(tiles, txt_grad, img_grad)


def shards(img_emb, txt_feat, txt_head, log_scale, bias):
    tiles, txt_grad, img_grad = main_call(img_emb, txt_feat, txt_head, log_scale, bias)
    head_grad, txt_grad, img_grad = final_call(tiles, txt_grad, img_grad)
    return (img_grad, txt_grad, head_grad)


def solution(mesh):
    return jax.shard_map(
        shards,
        mesh=mesh,
        in_specs=(P("batch", None), P("batch", None), P(), P(), P()),
        out_specs=(P("batch", None), P("batch", None), P()),
        check_vma=False,
    )
```

```python
import functools

import jax
import jax.numpy as jnp
from jax import lax
from jax.experimental import pallas as pl
from jax.experimental.pallas import tpu as pltpu
from jax.sharding import PartitionSpec as P

MESH = pl.DeviceIdType.MESH
F32 = jnp.float32
BF16 = jnp.bfloat16
ZS, XS, YS, CS = 8, 4, 4, 2
XY = XS * YS
E = 1152
ROWS = 512
HALF = E // 2
COLS = E // 128
UNITS = HALF // 16
NT = 328


def coords(me):
    return (me // (XS * YS * CS), (me // (YS * CS)) % XS, (me // CS) % YS, me % CS)


def device(z, x, y, c):
    return ((z * XS + x) * YS + y) * CS + c


def xy_member(me, d):
    z, x, y, c = coords(me)
    x = (x + d // YS) % XS
    y = (y + d % YS) % YS
    return (device(z, x, y, c), x * YS + y)


def xy_source(me, d):
    z, x, y, c = coords(me)
    return ((x + XS - d // YS) % XS) * YS + (y + YS - d % YS) % YS


def z_member(me, d):
    z, x, y, c = coords(me)
    z = (z + d) % ZS
    return (device(z, x, y, c), z)


def z_source(me, d):
    return (coords(me)[0] + ZS - d) % ZS


def other_core(me):
    return me + 1 - 2 * (me % CS)


def far_device(me):
    ring = ZS * XS * YS * CS
    return lax.rem(me + ring - 1 + 2 * (me % CS), ring)


def remote(src, dst, ssem, rsem, to):
    return pltpu.make_async_remote_copy(
        src_ref=src, dst_ref=dst, send_sem=ssem, recv_sem=rsem,
        device_id=(to,), device_id_type=MESH,
    )


def each(lo, hi, body):
    def step(i, carry):
        body(i)
        return carry

    lax.fori_loop(lo, hi, step, 0)


class Names:
    pass


XY_AXIS = (XY, xy_member, xy_source)
Z_AXIS = (ZS, z_member, z_source)


class Stream:
    def __init__(self, name, start, per, first, second):
        self.name = name
        self.start = start
        self.per = per
        self.first = first
        self.second = second

    def scratch(self):
        n, m = self.first[0], self.second[0]
        return {
            self.name + "_got": pltpu.VMEM((n, self.per, 16, 128), BF16),
            self.name + "_part": pltpu.VMEM((m, 16, 128), BF16),
            self.name + "_got2": pltpu.VMEM((m, 1, 16, 128), BF16),
            self.name + "_sum": pltpu.VMEM((m, 16, 128), BF16),
            self.name + "_send": pltpu.SemaphoreType.DMA((5, XY)),
            self.name + "_recv": pltpu.SemaphoreType.DMA((5, XY)),
        }

    def bind(self, me, w, out, s):
        self.me, self.w, self.out = me, w, out
        self.got, self.part, self.got2, self.sum, self.send, self.recv = (
            getattr(s, self.name + "_" + kind) for kind in ("got", "part", "got2", "sum", "send", "recv")
        )
        self.c = coords(me)[3]
        self.p = self.first[1](me, 0)[1]
        self.q = self.second[1](me, 0)[1]

    def copy(self, phase, src, dst, d, to):
        return remote(src, dst, self.send.at[phase, d], self.recv.at[phase, d], to)

    def scatter(self, d):
        to, q = self.first[1](self.me, d)
        return self.copy(0, self.w.at[pl.ds(self.start + q * self.per, self.per)], self.got.at[d], d, to)

    def scatter2(self, d):
        to, q = self.second[1](self.me, d)
        return self.copy(1, self.part.at[pl.ds(q, 1)], self.got2.at[d], d, to)

    def gather2(self, d):
        to, q = self.second[1](self.me, d)
        here = self.sum.at[pl.ds(self.q, 1)]
        return self.copy(2, here, here, d, to)

    def piece(self, q):
        return self.out.at[self.c, pl.ds(self.start + q * self.per, self.per)]

    def gather(self, d):
        to, q = self.first[1](self.me, d)
        return self.copy(3, self.sum.at[pl.ds(0, self.per)], self.piece(self.p), d, to)

    def own(self):
        return pltpu.make_async_copy(self.sum.at[pl.ds(0, self.per)], self.piece(self.p), self.send.at[3, 0])

    def hand(self, d):
        here = self.piece(self.first[2](self.me, d))
        return self.copy(4, here, here, d, other_core(self.me))

    def start_scatter(self):
        each(1, self.first[0], lambda d: self.scatter(d).start())

    def start_scatter2(self):
        each(1, self.first[0], lambda d: self.scatter(d).wait_recv())

        def add(i):
            total = self.w[self.start + self.p * self.per + i].astype(F32)
            total += jnp.sum(self.got[1:, i].astype(F32), axis=0)
            self.part[i] = total.astype(BF16)

        each(0, self.per, add)
        m = self.second[0]
        if m > self.per:
            self.part[self.per:] = jnp.zeros((m - self.per, 16, 128), BF16)
        each(1, m, lambda d: self.scatter2(d).start())

    def start_gather2(self):
        m = self.second[0]
        each(1, m, lambda d: self.scatter2(d).wait_recv())
        total = self.part[self.q].astype(F32) + jnp.sum(self.got2[1:, 0].astype(F32), axis=0)
        self.sum[self.q] = total.astype(BF16)
        each(1, m, lambda d: self.gather2(d).start())

    def start_gather(self):
        each(1, self.second[0], lambda d: self.gather2(d).wait_recv())
        each(1, self.first[0], lambda d: self.gather(d).start())
        self.own().start()

    def pass_own(self):
        self.own().wait()
        self.hand(0).start()

    def pass_on(self):
        def move(d):
            self.gather(d).wait_recv()
            self.hand(d).start()

        each(1, self.first[0], move)

    def finish(self):
        n, m = self.first[0], self.second[0]
        each(1, n, lambda d: self.scatter(d).wait_send())
        each(1, m, lambda d: self.scatter2(d).wait_send())
        each(1, m, lambda d: self.gather2(d).wait_send())
        each(1, n, lambda d: self.gather(d).wait_send())
        each(0, n, lambda d: self.hand(d).wait())


def streams():
    return (
        Stream("a1", 0, 7, XY_AXIS, Z_AXIS),
        Stream("b1", 112, 6, Z_AXIS, XY_AXIS),
        Stream("a2", 160, 7, XY_AXIS, Z_AXIS),
        Stream("b2", 272, 7, Z_AXIS, XY_AXIS),
    )


def greet_all(me):
    barrier = pltpu.get_barrier_semaphore()

    def greet(to):
        pl.semaphore_signal(barrier, inc=1, device_id=(to,), device_id_type=MESH)

    greet(far_device(me))
    greet(other_core(me))
    each(1, XY, lambda d: greet(xy_member(me, d)[0]))
    each(1, ZS, lambda d: greet(z_member(me, d)[0]))
    return barrier


RC = 128
EARLY = 256
NC = ROWS // RC
CW = 384
TAIL = 256
HB = 288


def rows_at(start, size):
    return pl.ds(pl.multiple_of(start, size), size)


def dot_nt(a, b):
    return lax.dot_general(a, b, (((1,), (1,)), ((), ())), preferred_element_type=F32)


def dot_nn(a, b):
    return jnp.dot(a, b, preferred_element_type=F32)


def unit_of(values):
    rinv = lax.rsqrt(jnp.sum(values * values, axis=-1, keepdims=True) + 1e-06)
    return (values * rinv, rinv)


def own_diagonal(shape):
    row = lax.broadcasted_iota(jnp.int32, shape, 0)
    return lax.broadcasted_iota(jnp.int32, shape, 1) == row


def across(total, unit, rinv):
    along = jnp.sum(unit * total, axis=-1, keepdims=True)
    return ((total - unit * along) * rinv).astype(BF16)


def main_kernel(img_hbm, feat_hbm, head_hbm, scale_ref, bias_ref, tiles, txt_out, img_out, *scratch):
    me = lax.axis_index("batch")
    c = me % CS
    near = other_core(me)
    far = far_device(me)
    s = Names()
    for name, ref in zip(list(MAIN_SCRATCH), scratch):
        setattr(s, name, ref)
    a1, b1, a2, b2 = lines = streams()
    for line in lines:
        line.bind(me, s.w, tiles, s)
    img_in = pltpu.make_async_copy(img_hbm, s.img, s.ins.at[0])
    feat_in = pltpu.make_async_copy(feat_hbm, s.feat, s.ins.at[1])
    head_in = pltpu.make_async_copy(head_hbm, s.head, s.ins.at[2])
    img_in.start()
    feat_in.start()
    head_in.start()
    barrier = greet_all(me)
    half = 0.5 * jnp.exp(jnp.full((1, 1), scale_ref[0], F32))
    shift = 0.5 * jnp.full((1, 1), bias_ref[0], F32)

    def weights(left, right, diagonal=False):
        weight = jnp.tanh(dot_nt(left, right) * half + shift) * half + half
        if diagonal:
            weight = weight - jnp.where(own_diagonal(weight.shape), 2.0 * half, 0.0)
        return weight.astype(BF16)

    def img_far(j):
        start, size = ((0, 2 * RC), (2 * RC, RC), (3 * RC, RC))[j]
        return remote(s.imgs.at[pl.ds(start, size)], s.imgs.at[pl.ds(2 * ROWS + start, size)],
                      s.es.at[j], s.er.at[j], far)

    def txt_far(j):
        start, size = ((0, EARLY), (EARLY, ROWS - EARLY))[j]
        return remote(s.txts.at[pl.ds(start, size)], s.txts.at[pl.ds(2 * ROWS + start, size)],
                      s.es.at[NC + j], s.er.at[NC + j], far)

    n = 2 * NC
    img_near = remote(s.imgs.at[pl.ds(0, ROWS)], s.imgs.at[pl.ds(ROWS, ROWS)], s.es.at[n], s.er.at[n], near)
    txt_near = remote(s.txts.at[pl.ds(0, ROWS)], s.txts.at[pl.ds(ROWS, ROWS)], s.es.at[n + 1], s.er.at[n + 1], near)
    theirs = rows_at((1 - c) * HALF, HALF)
    feat_near = remote(s.feat_t.at[theirs], s.feat_nbr, s.es.at[n + 2], s.er.at[n + 2], near)

    def hid_near(k):
        return remote(s.hid.at[pl.ds(k * TAIL, TAIL)], s.hid.at[pl.ds(ROWS + k * TAIL, TAIL)],
                      s.es.at[n + 3 + k], s.er.at[n + 3 + k], near)

    img_in.wait()

    def unit_images(j):
        at = pl.ds(j * RC, RC)
        unit, rinv = unit_of(s.img[at, :].astype(F32))
        s.imgs[at, :] = unit.astype(BF16)
        s.img_rinv[at, :] = rinv

    unit_images(0)
    unit_images(1)
    pl.semaphore_wait(barrier, XY + ZS)
    img_far(0).start()
    unit_images(2)
    img_far(1).start()
    unit_images(3)
    img_far(2).start()
    img_near.start()
    feat_in.wait()
    head_in.wait()
    s.txt_unit[...] = dot_nn(s.feat[...], s.head[...])

    def unit_texts(j):
        at = rows_at(j * RC, RC)
        unit, rinv = unit_of(s.txt_unit[at, :])
        s.txt_unit[at, :] = unit
        s.txts[at, :] = unit.astype(BF16)
        s.txt_rinv[at, :] = rinv

    each(0, NC, unit_texts)
    txt_near.start()
    txt_far(0).start()

    own = pl.ds(0, ROWS)
    nbr = pl.ds(ROWS, ROWS)
    s.wt[:, 0:ROWS] = weights(s.txts[own, :], s.imgs[own, :], True)

    def flip(i):
        cols = rows_at(i * 128, 128)
        s.feat_t[cols, :] = s.feat[:, cols].T

    each(0, COLS, flip)
    feat_near.start()
    img_near.wait_recv()
    s.wt[:, ROWS:2 * ROWS] = weights(s.txts[own, :], s.imgs[nbr, :])

    def sums_of(sums, block, first, size, add):
        def columns(i):
            cols = rows_at(i * CW, CW)
            value = dot_nn(s.wt[:, first:first + size], block[first:first + size, cols])
            sums[:, cols] = sums[:, cols] + value if add else value

        each(0, E // CW, columns)

    sums_of(s.text_sum, s.imgs, 0, 2 * ROWS, False)
    base = 2 * ROWS
    img_far(0).wait_recv()
    s.wt[:, base:base + 2 * RC] = weights(s.txts[own, :], s.imgs[pl.ds(base, 2 * RC), :])
    img_far(1).wait_recv()
    s.wt[:, base + 2 * RC:base + 3 * RC] = weights(s.txts[own, :], s.imgs[pl.ds(base + 2 * RC, RC), :])
    sums_of(s.text_sum, s.imgs, base, 3 * RC, True)
    img_far(2).wait_recv()
    last = pl.ds(base + 3 * RC, RC)
    for k in range(ROWS // TAIL):
        at = pl.ds(k * TAIL, TAIL)
        weight = weights(s.txts[at, :], s.imgs[last, :])
        total = s.text_sum[at, :] + dot_nn(weight, s.imgs[last, :])
        s.hid[at, :] = across(total, s.txt_unit[at, :], s.txt_rinv[at, :])
        hid_near(k).start()

    def head_own(i):
        mine = s.feat_t[rows_at(c * HALF + i * HB, HB), :]
        s.head_sum[rows_at(i * HB, HB), :] = dot_nn(mine, s.hid[own, :])

    each(0, HALF // HB, head_own)
    feat_near.wait_recv()
    for k in range(ROWS // TAIL):
        hid_near(k).wait_recv()

    def head_both(i):
        at = pl.ds(i * HB, HB)
        value = s.head_sum[at, :] + dot_nn(s.feat_nbr[at, :], s.hid[nbr, :])
        value = value.astype(BF16)
        for r in range(HB // 16):
            for col in range(COLS):
                s.w[(i * HB // 16 + r) * COLS + col] = value[r * 16:(r + 1) * 16, col * 128:(col + 1) * 128]

    head_both(0)
    b1.start_scatter()
    a1.start_scatter()
    head_both(1)
    s.w[UNITS * COLS:] = jnp.zeros((NT - UNITS * COLS, 16, 128), BF16)
    b2.start_scatter()
    a2.start_scatter()

    txt_write = pltpu.make_async_copy(s.txt_grad, txt_out, s.outs.at[0])
    img_write = pltpu.make_async_copy(s.img_grad, img_out, s.outs.at[1])

    def text_grads(i):
        cols = rows_at(i * CW, CW)
        s.txt_grad[:, cols] = dot_nt(s.hid[own, :], s.head[cols, :]).astype(BF16)

    each(0, E // CW, text_grads)
    txt_write.start()
    s.wt[:, 0:ROWS] = weights(s.imgs[own, :], s.txts[own, :], True)
    txt_near.wait_recv()
    s.wt[:, ROWS:2 * ROWS] = weights(s.imgs[own, :], s.txts[nbr, :])
    sums_of(s.img_sum, s.txts, 0, 2 * ROWS, False)

    def image_far(j):
        start, size = ((0, EARLY), (EARLY, ROWS - EARLY))[j]
        txt_far(j).wait_recv()
        s.wt[:, base + start:base + start + size] = weights(s.imgs[own, :], s.txts[pl.ds(base + start, size), :])
        sums_of(s.img_sum, s.txts, base + start, size, True)

    image_far(0)

    for line in (b1, a1, b2, a2):
        line.start_scatter2()
    txt_far(1).start()
    for line in (b1, a1, b2, a2):
        line.start_gather2()
    for line in (b1, a1, b2, a2):
        line.start_gather()
    for line in (b1, a1, b2, a2):
        line.pass_own()
    b1.pass_on()
    a1.pass_on()
    image_far(1)
    def image_grads(j):
        at = rows_at(j * RC, RC)
        rinv = s.img_rinv[at, :]
        s.img_grad[at, :] = across(s.img_sum[at, :], s.img[at, :].astype(F32) * rinv, rinv)

    each(0, NC, image_grads)
    img_write.start()
    b2.pass_on()
    a2.pass_on()
    for line in lines:
        line.finish()
    for j in range(3):
        img_far(j).wait_send()
    for j in range(2):
        txt_far(j).wait_send()
    img_near.wait_send()
    txt_near.wait_send()
    feat_near.wait_send()
    for k in range(ROWS // TAIL):
        hid_near(k).wait_send()
    txt_write.wait()
    img_write.wait()


MAIN_SCRATCH = dict(
    img=pltpu.VMEM((ROWS, E), BF16),
    feat=pltpu.VMEM((ROWS, E), BF16),
    head=pltpu.VMEM((E, E), BF16),
    imgs=pltpu.VMEM((3 * ROWS, E), BF16),
    txts=pltpu.VMEM((3 * ROWS, E), BF16),
    wt=pltpu.VMEM((ROWS, 3 * ROWS), BF16),
    img_rinv=pltpu.VMEM((ROWS, 1), F32),
    txt_rinv=pltpu.VMEM((ROWS, 1), F32),
    txt_unit=pltpu.VMEM((ROWS, E), F32),
    text_sum=pltpu.VMEM((ROWS, E), F32),
    img_sum=pltpu.VMEM((ROWS, E), F32),
    hid=pltpu.VMEM((2 * ROWS, E), BF16),
    feat_t=pltpu.VMEM((E, ROWS), BF16),
    feat_nbr=pltpu.VMEM((HALF, ROWS), BF16),
    head_sum=pltpu.VMEM((HALF, E), F32),
    w=pltpu.VMEM((NT, 16, 128), BF16),
    txt_grad=pltpu.VMEM((ROWS, E), BF16),
    img_grad=pltpu.VMEM((ROWS, E), BF16),
    ins=pltpu.SemaphoreType.DMA((3,)),
    outs=pltpu.SemaphoreType.DMA((2,)),
    es=pltpu.SemaphoreType.DMA((2 * NC + 5,)),
    er=pltpu.SemaphoreType.DMA((2 * NC + 5,)),
)
for line in streams():
    MAIN_SCRATCH.update(line.scratch())


def main_call(img_emb, txt_feat, txt_head, log_scale, bias):
    return pl.pallas_call(
        main_kernel,
        out_shape=(
            jax.ShapeDtypeStruct((CS, NT, 16, 128), BF16),
            jax.ShapeDtypeStruct((ROWS, E), BF16),
            jax.ShapeDtypeStruct((ROWS, E), BF16),
        ),
        in_specs=[pl.BlockSpec(memory_space=pl.ANY)] * 3 + [pl.BlockSpec(memory_space=pltpu.SMEM)] * 2,
        out_specs=[pl.BlockSpec(memory_space=pl.ANY)] * 3,
        scratch_shapes=list(MAIN_SCRATCH.values()),
        compiler_params=pltpu.CompilerParams(
            collective_id=0, has_side_effects=True, vmem_limit_bytes=56 << 20
        ),
        name="main",
    )(img_emb, txt_feat, txt_head, log_scale, bias)


LAY = 96


def final_kernel(tiles_hbm, txt_hbm, img_hbm, head_out, txt_out, img_out, tiles, head, txt, img, sems):
    txt_in = pltpu.make_async_copy(txt_hbm, txt, sems.at[0])
    img_in = pltpu.make_async_copy(img_hbm, img, sems.at[1])
    txt_back = pltpu.make_async_copy(txt, txt_out, sems.at[2])
    img_back = pltpu.make_async_copy(img, img_out, sems.at[3])
    per = LAY // 16 * COLS
    blocks = HALF // LAY

    def read(i):
        at = pl.ds((i % blocks) * per, per)
        return pltpu.make_async_copy(tiles_hbm.at[i // blocks, at], tiles.at[i // blocks, at], sems.at[4 + i])

    def write(i):
        at = rows_at(i * LAY, LAY)
        return pltpu.make_async_copy(head.at[at], head_out.at[at], sems.at[4 + CS * blocks + i])

    each(0, CS * blocks, lambda i: read(i).start())
    txt_in.start()
    img_in.start()

    def lay(i):
        read(i).wait()
        for r in range(LAY // 16):
            for col in range(COLS):
                value = tiles[i // blocks, (i % blocks) * per + r * COLS + col]
                head[pl.ds(pl.multiple_of(i * LAY + r * 16, 16), 16), col * 128:(col + 1) * 128] = value.astype(F32)
        write(i).start()

    each(0, CS * blocks, lay)
    txt_in.wait()
    txt_back.start()
    img_in.wait()
    img_back.start()
    each(0, CS * blocks, lambda i: write(i).wait())
    txt_back.wait()
    img_back.wait()


def final_call(tiles, txt_grad, img_grad):
    return pl.pallas_call(
        final_kernel,
        out_shape=(
            jax.ShapeDtypeStruct((E, E), F32),
            jax.ShapeDtypeStruct((ROWS, E), BF16),
            jax.ShapeDtypeStruct((ROWS, E), BF16),
        ),
        in_specs=[pl.BlockSpec(memory_space=pl.ANY)] * 3,
        out_specs=[pl.BlockSpec(memory_space=pl.ANY)] * 3,
        scratch_shapes=[
            pltpu.VMEM((CS, NT, 16, 128), BF16),
            pltpu.VMEM((E, E), F32),
            pltpu.VMEM((ROWS, E), BF16),
            pltpu.VMEM((ROWS, E), BF16),
            pltpu.SemaphoreType.DMA((4 + 2 * CS * HALF // LAY,)),
        ],
        compiler_params=pltpu.CompilerParams(vmem_limit_bytes=56 << 20),
        name="final",
    )(tiles, txt_grad, img_grad)


def shards(img_emb, txt_feat, txt_head, log_scale, bias):
    tiles, txt_grad, img_grad = main_call(img_emb, txt_feat, txt_head, log_scale, bias)
    head_grad, txt_grad, img_grad = final_call(tiles, txt_grad, img_grad)
    return (img_grad, txt_grad, head_grad)


def solution(mesh):
    return jax.shard_map(
        shards,
        mesh=mesh,
        in_specs=(P("batch", None), P("batch", None), P(), P(), P()),
        out_specs=(P("batch", None), P("batch", None), P()),
        check_vma=False,
    )
```

```python
import functools

import jax
import jax.numpy as jnp
from jax import lax
from jax.experimental import pallas as pl
from jax.experimental.pallas import tpu as pltpu
from jax.sharding import PartitionSpec as P

MESH = pl.DeviceIdType.MESH
F32 = jnp.float32
BF16 = jnp.bfloat16
ZS, XS, YS, CS = 8, 4, 4, 2
XY = XS * YS
E = 1152
ROWS = 512
HALF = E // 2
COLS = E // 128
UNITS = HALF // 16
NT = 328


def coords(me):
    return (me // (XS * YS * CS), (me // (YS * CS)) % XS, (me // CS) % YS, me % CS)


def device(z, x, y, c):
    return ((z * XS + x) * YS + y) * CS + c


def xy_member(me, d):
    z, x, y, c = coords(me)
    x = (x + d // YS) % XS
    y = (y + d % YS) % YS
    return (device(z, x, y, c), x * YS + y)


def xy_source(me, d):
    z, x, y, c = coords(me)
    return ((x + XS - d // YS) % XS) * YS + (y + YS - d % YS) % YS


def z_member(me, d):
    z, x, y, c = coords(me)
    z = (z + d) % ZS
    return (device(z, x, y, c), z)


def z_source(me, d):
    return (coords(me)[0] + ZS - d) % ZS


def other_core(me):
    return me + 1 - 2 * (me % CS)


def far_device(me):
    ring = ZS * XS * YS * CS
    return lax.rem(me + ring - 1 + 2 * (me % CS), ring)


def remote(src, dst, ssem, rsem, to):
    return pltpu.make_async_remote_copy(
        src_ref=src, dst_ref=dst, send_sem=ssem, recv_sem=rsem,
        device_id=(to,), device_id_type=MESH,
    )


def each(lo, hi, body):
    def step(i, carry):
        body(i)
        return carry

    lax.fori_loop(lo, hi, step, 0)


class Names:
    pass


XY_AXIS = (XY, xy_member, xy_source)
Z_AXIS = (ZS, z_member, z_source)


class Stream:
    def __init__(self, name, start, per, first, second):
        self.name = name
        self.start = start
        self.per = per
        self.first = first
        self.second = second

    def scratch(self):
        n, m = self.first[0], self.second[0]
        return {
            self.name + "_got": pltpu.VMEM((n, self.per, 16, 128), BF16),
            self.name + "_part": pltpu.VMEM((m, 16, 128), BF16),
            self.name + "_got2": pltpu.VMEM((m, 1, 16, 128), BF16),
            self.name + "_sum": pltpu.VMEM((m, 16, 128), BF16),
            self.name + "_send": pltpu.SemaphoreType.DMA((5, XY)),
            self.name + "_recv": pltpu.SemaphoreType.DMA((5, XY)),
        }

    def bind(self, me, w, out, s):
        self.me, self.w, self.out = me, w, out
        self.got, self.part, self.got2, self.sum, self.send, self.recv = (
            getattr(s, self.name + "_" + kind) for kind in ("got", "part", "got2", "sum", "send", "recv")
        )
        self.c = coords(me)[3]
        self.p = self.first[1](me, 0)[1]
        self.q = self.second[1](me, 0)[1]

    def copy(self, phase, src, dst, d, to):
        return remote(src, dst, self.send.at[phase, d], self.recv.at[phase, d], to)

    def scatter(self, d):
        to, q = self.first[1](self.me, d)
        return self.copy(0, self.w.at[pl.ds(self.start + q * self.per, self.per)], self.got.at[d], d, to)

    def scatter2(self, d):
        to, q = self.second[1](self.me, d)
        return self.copy(1, self.part.at[pl.ds(q, 1)], self.got2.at[d], d, to)

    def gather2(self, d):
        to, q = self.second[1](self.me, d)
        here = self.sum.at[pl.ds(self.q, 1)]
        return self.copy(2, here, here, d, to)

    def piece(self, q):
        return self.out.at[self.c, pl.ds(self.start + q * self.per, self.per)]

    def gather(self, d):
        to, q = self.first[1](self.me, d)
        return self.copy(3, self.sum.at[pl.ds(0, self.per)], self.piece(self.p), d, to)

    def own(self):
        return pltpu.make_async_copy(self.sum.at[pl.ds(0, self.per)], self.piece(self.p), self.send.at[3, 0])

    def hand(self, d):
        here = self.piece(self.first[2](self.me, d))
        return self.copy(4, here, here, d, other_core(self.me))

    def start_scatter(self):
        each(1, self.first[0], lambda d: self.scatter(d).start())

    def start_scatter2(self):
        each(1, self.first[0], lambda d: self.scatter(d).wait_recv())

        def add(i):
            total = self.w[self.start + self.p * self.per + i].astype(F32)
            total += jnp.sum(self.got[1:, i].astype(F32), axis=0)
            self.part[i] = total.astype(BF16)

        each(0, self.per, add)
        m = self.second[0]
        if m > self.per:
            self.part[self.per:] = jnp.zeros((m - self.per, 16, 128), BF16)
        each(1, m, lambda d: self.scatter2(d).start())

    def start_gather2(self):
        m = self.second[0]
        each(1, m, lambda d: self.scatter2(d).wait_recv())
        total = self.part[self.q].astype(F32) + jnp.sum(self.got2[1:, 0].astype(F32), axis=0)
        self.sum[self.q] = total.astype(BF16)
        each(1, m, lambda d: self.gather2(d).start())

    def start_gather(self):
        each(1, self.second[0], lambda d: self.gather2(d).wait_recv())
        each(1, self.first[0], lambda d: self.gather(d).start())
        self.own().start()

    def pass_own(self):
        self.own().wait()
        self.hand(0).start()

    def pass_on(self):
        def move(d):
            self.gather(d).wait_recv()
            self.hand(d).start()

        each(1, self.first[0], move)

    def finish(self):
        n, m = self.first[0], self.second[0]
        each(1, n, lambda d: self.scatter(d).wait_send())
        each(1, m, lambda d: self.scatter2(d).wait_send())
        each(1, m, lambda d: self.gather2(d).wait_send())
        each(1, n, lambda d: self.gather(d).wait_send())
        each(0, n, lambda d: self.hand(d).wait())


def streams():
    return (
        Stream("a1", 0, 7, XY_AXIS, Z_AXIS),
        Stream("b1", 112, 6, Z_AXIS, XY_AXIS),
        Stream("a2", 160, 7, XY_AXIS, Z_AXIS),
        Stream("b2", 272, 7, Z_AXIS, XY_AXIS),
    )


def greet_all(me):
    barrier = pltpu.get_barrier_semaphore()

    def greet(to):
        pl.semaphore_signal(barrier, inc=1, device_id=(to,), device_id_type=MESH)

    greet(far_device(me))
    greet(other_core(me))
    each(1, XY, lambda d: greet(xy_member(me, d)[0]))
    each(1, ZS, lambda d: greet(z_member(me, d)[0]))
    return barrier


RC = 128
EARLY = 320
NC = ROWS // RC
CW = 384
TAIL = 256
HB = 288


def rows_at(start, size):
    return pl.ds(pl.multiple_of(start, size), size)


def dot_nt(a, b):
    return lax.dot_general(a, b, (((1,), (1,)), ((), ())), preferred_element_type=F32)


def dot_nn(a, b):
    return jnp.dot(a, b, preferred_element_type=F32)


def unit_of(values):
    rinv = lax.rsqrt(jnp.sum(values * values, axis=-1, keepdims=True) + 1e-06)
    return (values * rinv, rinv)


def own_diagonal(shape):
    row = lax.broadcasted_iota(jnp.int32, shape, 0)
    return lax.broadcasted_iota(jnp.int32, shape, 1) == row


def across(total, unit, rinv):
    along = jnp.sum(unit * total, axis=-1, keepdims=True)
    return ((total - unit * along) * rinv).astype(BF16)


def main_kernel(img_hbm, feat_hbm, head_hbm, scale_ref, bias_ref, tiles, txt_out, img_out, *scratch):
    me = lax.axis_index("batch")
    c = me % CS
    near = other_core(me)
    far = far_device(me)
    s = Names()
    for name, ref in zip(list(MAIN_SCRATCH), scratch):
        setattr(s, name, ref)
    a1, b1, a2, b2 = lines = streams()
    for line in lines:
        line.bind(me, s.w, tiles, s)
    img_in = pltpu.make_async_copy(img_hbm, s.img, s.ins.at[0])
    feat_in = pltpu.make_async_copy(feat_hbm, s.feat, s.ins.at[1])
    head_in = pltpu.make_async_copy(head_hbm, s.head, s.ins.at[2])
    img_in.start()
    feat_in.start()
    head_in.start()
    barrier = greet_all(me)
    half = 0.5 * jnp.exp(jnp.full((1, 1), scale_ref[0], F32))
    shift = 0.5 * jnp.full((1, 1), bias_ref[0], F32)

    def weights(left, right, diagonal=False):
        weight = jnp.tanh(dot_nt(left, right) * half + shift) * half + half
        if diagonal:
            weight = weight - jnp.where(own_diagonal(weight.shape), 2.0 * half, 0.0)
        return weight.astype(BF16)

    def img_far(j):
        start, size = ((0, 2 * RC), (2 * RC, RC), (3 * RC, RC))[j]
        return remote(s.imgs.at[pl.ds(start, size)], s.imgs.at[pl.ds(2 * ROWS + start, size)],
                      s.es.at[j], s.er.at[j], far)

    def txt_far(j):
        start, size = ((0, EARLY), (EARLY, ROWS - EARLY))[j]
        return remote(s.txts.at[pl.ds(start, size)], s.txts.at[pl.ds(2 * ROWS + start, size)],
                      s.es.at[NC + j], s.er.at[NC + j], far)

    n = 2 * NC
    img_near = remote(s.imgs.at[pl.ds(0, ROWS)], s.imgs.at[pl.ds(ROWS, ROWS)], s.es.at[n], s.er.at[n], near)
    txt_near = remote(s.txts.at[pl.ds(0, ROWS)], s.txts.at[pl.ds(ROWS, ROWS)], s.es.at[n + 1], s.er.at[n + 1], near)
    theirs = rows_at((1 - c) * HALF, HALF)
    feat_near = remote(s.feat_t.at[theirs], s.feat_nbr, s.es.at[n + 2], s.er.at[n + 2], near)

    def hid_near(k):
        return remote(s.hid.at[pl.ds(k * TAIL, TAIL)], s.hid.at[pl.ds(ROWS + k * TAIL, TAIL)],
                      s.es.at[n + 3 + k], s.er.at[n + 3 + k], near)

    img_in.wait()

    def unit_images(j):
        at = pl.ds(j * RC, RC)
        unit, rinv = unit_of(s.img[at, :].astype(F32))
        s.imgs[at, :] = unit.astype(BF16)
        s.img_rinv[at, :] = rinv

    unit_images(0)
    unit_images(1)
    pl.semaphore_wait(barrier, XY + ZS)
    img_far(0).start()
    unit_images(2)
    img_far(1).start()
    unit_images(3)
    img_far(2).start()
    img_near.start()
    feat_in.wait()
    head_in.wait()
    s.txt_unit[...] = dot_nn(s.feat[...], s.head[...])

    def unit_texts(j):
        at = rows_at(j * RC, RC)
        unit, rinv = unit_of(s.txt_unit[at, :])
        s.txt_unit[at, :] = unit
        s.txts[at, :] = unit.astype(BF16)
        s.txt_rinv[at, :] = rinv

    each(0, NC, unit_texts)
    txt_near.start()
    txt_far(0).start()

    own = pl.ds(0, ROWS)
    nbr = pl.ds(ROWS, ROWS)
    s.wt[:, 0:ROWS] = weights(s.txts[own, :], s.imgs[own, :], True)

    def flip(i):
        cols = rows_at(i * 128, 128)
        s.feat_t[cols, :] = s.feat[:, cols].T

    each(0, COLS, flip)
    feat_near.start()
    img_near.wait_recv()
    s.wt[:, ROWS:2 * ROWS] = weights(s.txts[own, :], s.imgs[nbr, :])

    def sums_of(sums, block, first, size, add):
        def columns(i):
            cols = rows_at(i * CW, CW)
            value = dot_nn(s.wt[:, first:first + size], block[first:first + size, cols])
            sums[:, cols] = sums[:, cols] + value if add else value

        each(0, E // CW, columns)

    sums_of(s.text_sum, s.imgs, 0, 2 * ROWS, False)
    base = 2 * ROWS
    img_far(0).wait_recv()
    s.wt[:, base:base + 2 * RC] = weights(s.txts[own, :], s.imgs[pl.ds(base, 2 * RC), :])
    img_far(1).wait_recv()
    s.wt[:, base + 2 * RC:base + 3 * RC] = weights(s.txts[own, :], s.imgs[pl.ds(base + 2 * RC, RC), :])
    sums_of(s.text_sum, s.imgs, base, 3 * RC, True)
    img_far(2).wait_recv()
    last = pl.ds(base + 3 * RC, RC)
    for k in range(ROWS // TAIL):
        at = pl.ds(k * TAIL, TAIL)
        weight = weights(s.txts[at, :], s.imgs[last, :])
        total = s.text_sum[at, :] + dot_nn(weight, s.imgs[last, :])
        s.hid[at, :] = across(total, s.txt_unit[at, :], s.txt_rinv[at, :])
        hid_near(k).start()

    def head_own(i):
        mine = s.feat_t[rows_at(c * HALF + i * HB, HB), :]
        s.head_sum[rows_at(i * HB, HB), :] = dot_nn(mine, s.hid[own, :])

    each(0, HALF // HB, head_own)
    feat_near.wait_recv()
    for k in range(ROWS // TAIL):
        hid_near(k).wait_recv()

    def head_both(i):
        at = pl.ds(i * HB, HB)
        value = s.head_sum[at, :] + dot_nn(s.feat_nbr[at, :], s.hid[nbr, :])
        value = value.astype(BF16)
        for r in range(HB // 16):
            for col in range(COLS):
                s.w[(i * HB // 16 + r) * COLS + col] = value[r * 16:(r + 1) * 16, col * 128:(col + 1) * 128]

    head_both(0)
    a1.start_scatter()
    b1.start_scatter()
    head_both(1)
    s.w[UNITS * COLS:] = jnp.zeros((NT - UNITS * COLS, 16, 128), BF16)
    a2.start_scatter()
    b2.start_scatter()

    txt_write = pltpu.make_async_copy(s.txt_grad, txt_out, s.outs.at[0])
    img_write = pltpu.make_async_copy(s.img_grad, img_out, s.outs.at[1])

    def text_grads(i):
        cols = rows_at(i * CW, CW)
        s.txt_grad[:, cols] = dot_nt(s.hid[own, :], s.head[cols, :]).astype(BF16)

    each(0, E // CW, text_grads)
    txt_write.start()
    s.wt[:, 0:ROWS] = weights(s.imgs[own, :], s.txts[own, :], True)
    txt_near.wait_recv()
    s.wt[:, ROWS:2 * ROWS] = weights(s.imgs[own, :], s.txts[nbr, :])
    sums_of(s.img_sum, s.txts, 0, 2 * ROWS, False)

    def image_far(j):
        start, size = ((0, EARLY), (EARLY, ROWS - EARLY))[j]
        txt_far(j).wait_recv()
        s.wt[:, base + start:base + start + size] = weights(s.imgs[own, :], s.txts[pl.ds(base + start, size), :])
        sums_of(s.img_sum, s.txts, base + start, size, True)

    image_far(0)

    for line in (b1, a1, b2, a2):
        line.start_scatter2()
    txt_far(1).start()
    for line in (b1, a1, b2, a2):
        line.start_gather2()
    for line in (b1, a1, b2, a2):
        line.start_gather()
    for line in (b1, a1, b2, a2):
        line.pass_own()
    b1.pass_on()
    a1.pass_on()
    image_far(1)
    def image_grads(j):
        at = rows_at(j * RC, RC)
        rinv = s.img_rinv[at, :]
        s.img_grad[at, :] = across(s.img_sum[at, :], s.img[at, :].astype(F32) * rinv, rinv)

    each(0, NC, image_grads)
    img_write.start()
    b2.pass_on()
    a2.pass_on()
    for line in lines:
        line.finish()
    for j in range(3):
        img_far(j).wait_send()
    for j in range(2):
        txt_far(j).wait_send()
    img_near.wait_send()
    txt_near.wait_send()
    feat_near.wait_send()
    for k in range(ROWS // TAIL):
        hid_near(k).wait_send()
    txt_write.wait()
    img_write.wait()


MAIN_SCRATCH = dict(
    img=pltpu.VMEM((ROWS, E), BF16),
    feat=pltpu.VMEM((ROWS, E), BF16),
    head=pltpu.VMEM((E, E), BF16),
    imgs=pltpu.VMEM((3 * ROWS, E), BF16),
    txts=pltpu.VMEM((3 * ROWS, E), BF16),
    wt=pltpu.VMEM((ROWS, 3 * ROWS), BF16),
    img_rinv=pltpu.VMEM((ROWS, 1), F32),
    txt_rinv=pltpu.VMEM((ROWS, 1), F32),
    txt_unit=pltpu.VMEM((ROWS, E), F32),
    text_sum=pltpu.VMEM((ROWS, E), F32),
    img_sum=pltpu.VMEM((ROWS, E), F32),
    hid=pltpu.VMEM((2 * ROWS, E), BF16),
    feat_t=pltpu.VMEM((E, ROWS), BF16),
    feat_nbr=pltpu.VMEM((HALF, ROWS), BF16),
    head_sum=pltpu.VMEM((HALF, E), F32),
    w=pltpu.VMEM((NT, 16, 128), BF16),
    txt_grad=pltpu.VMEM((ROWS, E), BF16),
    img_grad=pltpu.VMEM((ROWS, E), BF16),
    ins=pltpu.SemaphoreType.DMA((3,)),
    outs=pltpu.SemaphoreType.DMA((2,)),
    es=pltpu.SemaphoreType.DMA((2 * NC + 5,)),
    er=pltpu.SemaphoreType.DMA((2 * NC + 5,)),
)
for line in streams():
    MAIN_SCRATCH.update(line.scratch())


def main_call(img_emb, txt_feat, txt_head, log_scale, bias):
    return pl.pallas_call(
        main_kernel,
        out_shape=(
            jax.ShapeDtypeStruct((CS, NT, 16, 128), BF16),
            jax.ShapeDtypeStruct((ROWS, E), BF16),
            jax.ShapeDtypeStruct((ROWS, E), BF16),
        ),
        in_specs=[pl.BlockSpec(memory_space=pl.ANY)] * 3 + [pl.BlockSpec(memory_space=pltpu.SMEM)] * 2,
        out_specs=[pl.BlockSpec(memory_space=pl.ANY)] * 3,
        scratch_shapes=list(MAIN_SCRATCH.values()),
        compiler_params=pltpu.CompilerParams(
            collective_id=0, has_side_effects=True, vmem_limit_bytes=56 << 20
        ),
        name="main",
    )(img_emb, txt_feat, txt_head, log_scale, bias)


LAY = 288


def final_kernel(tiles_hbm, txt_hbm, img_hbm, head_out, txt_out, img_out, tiles, head, txt, img, sems):
    txt_in = pltpu.make_async_copy(txt_hbm, txt, sems.at[0])
    img_in = pltpu.make_async_copy(img_hbm, img, sems.at[1])
    txt_back = pltpu.make_async_copy(txt, txt_out, sems.at[2])
    img_back = pltpu.make_async_copy(img, img_out, sems.at[3])
    per = LAY // 16 * COLS
    blocks = HALF // LAY

    def read(i):
        at = pl.ds((i % blocks) * per, per)
        return pltpu.make_async_copy(tiles_hbm.at[i // blocks, at], tiles.at[i // blocks, at], sems.at[4 + i])

    def write(i):
        at = rows_at(i * LAY, LAY)
        return pltpu.make_async_copy(head.at[at], head_out.at[at], sems.at[4 + CS * blocks + i])

    each(0, CS * blocks, lambda i: read(i).start())
    txt_in.start()
    img_in.start()

    def lay(i):
        read(i).wait()
        for r in range(LAY // 16):
            for col in range(COLS):
                value = tiles[i // blocks, (i % blocks) * per + r * COLS + col]
                head[pl.ds(pl.multiple_of(i * LAY + r * 16, 16), 16), col * 128:(col + 1) * 128] = value.astype(F32)
        write(i).start()

    each(0, CS * blocks, lay)
    txt_in.wait()
    txt_back.start()
    img_in.wait()
    img_back.start()
    each(0, CS * blocks, lambda i: write(i).wait())
    txt_back.wait()
    img_back.wait()


def final_call(tiles, txt_grad, img_grad):
    return pl.pallas_call(
        final_kernel,
        out_shape=(
            jax.ShapeDtypeStruct((E, E), F32),
            jax.ShapeDtypeStruct((ROWS, E), BF16),
            jax.ShapeDtypeStruct((ROWS, E), BF16),
        ),
        in_specs=[pl.BlockSpec(memory_space=pl.ANY)] * 3,
        out_specs=[pl.BlockSpec(memory_space=pl.ANY)] * 3,
        scratch_shapes=[
            pltpu.VMEM((CS, NT, 16, 128), BF16),
            pltpu.VMEM((E, E), F32),
            pltpu.VMEM((ROWS, E), BF16),
            pltpu.VMEM((ROWS, E), BF16),
            pltpu.SemaphoreType.DMA((4 + 2 * CS * HALF // LAY,)),
        ],
        compiler_params=pltpu.CompilerParams(vmem_limit_bytes=56 << 20),
        name="final",
    )(tiles, txt_grad, img_grad)


def shards(img_emb, txt_feat, txt_head, log_scale, bias):
    tiles, txt_grad, img_grad = main_call(img_emb, txt_feat, txt_head, log_scale, bias)
    head_grad, txt_grad, img_grad = final_call(tiles, txt_grad, img_grad)
    return (img_grad, txt_grad, head_grad)


def solution(mesh):
    return jax.shard_map(
        shards,
        mesh=mesh,
        in_specs=(P("batch", None), P("batch", None), P(), P(), P()),
        out_specs=(P("batch", None), P("batch", None), P()),
        check_vma=False,
    )
```

```python
import functools

import jax
import jax.numpy as jnp
from jax import lax
from jax.experimental import pallas as pl
from jax.experimental.pallas import tpu as pltpu
from jax.sharding import PartitionSpec as P

MESH = pl.DeviceIdType.MESH
F32 = jnp.float32
BF16 = jnp.bfloat16
ZS, XS, YS, CS = 8, 4, 4, 2
XY = XS * YS
E = 1152
ROWS = 512
HALF = E // 2
COLS = E // 128
UNITS = HALF // 16
NT = 328


def coords(me):
    return (me // (XS * YS * CS), (me // (YS * CS)) % XS, (me // CS) % YS, me % CS)


def device(z, x, y, c):
    return ((z * XS + x) * YS + y) * CS + c


def xy_member(me, d):
    z, x, y, c = coords(me)
    x = (x + d // YS) % XS
    y = (y + d % YS) % YS
    return (device(z, x, y, c), x * YS + y)


def xy_source(me, d):
    z, x, y, c = coords(me)
    return ((x + XS - d // YS) % XS) * YS + (y + YS - d % YS) % YS


def z_member(me, d):
    z, x, y, c = coords(me)
    z = (z + d) % ZS
    return (device(z, x, y, c), z)


def z_source(me, d):
    return (coords(me)[0] + ZS - d) % ZS


def other_core(me):
    return me + 1 - 2 * (me % CS)


def far_device(me):
    ring = ZS * XS * YS * CS
    return lax.rem(me + ring - 1 + 2 * (me % CS), ring)


def remote(src, dst, ssem, rsem, to):
    return pltpu.make_async_remote_copy(
        src_ref=src, dst_ref=dst, send_sem=ssem, recv_sem=rsem,
        device_id=(to,), device_id_type=MESH,
    )


def each(lo, hi, body):
    def step(i, carry):
        body(i)
        return carry

    lax.fori_loop(lo, hi, step, 0)


class Names:
    pass


XY_AXIS = (XY, xy_member, xy_source)
Z_AXIS = (ZS, z_member, z_source)


class Stream:
    def __init__(self, name, start, per, first, second):
        self.name = name
        self.start = start
        self.per = per
        self.first = first
        self.second = second

    def scratch(self):
        n, m = self.first[0], self.second[0]
        return {
            self.name + "_got": pltpu.VMEM((n, self.per, 16, 128), BF16),
            self.name + "_part": pltpu.VMEM((m, 16, 128), BF16),
            self.name + "_got2": pltpu.VMEM((m, 1, 16, 128), BF16),
            self.name + "_sum": pltpu.VMEM((m, 16, 128), BF16),
            self.name + "_send": pltpu.SemaphoreType.DMA((5, XY)),
            self.name + "_recv": pltpu.SemaphoreType.DMA((5, XY)),
        }

    def bind(self, me, w, out, s):
        self.me, self.w, self.out = me, w, out
        self.got, self.part, self.got2, self.sum, self.send, self.recv = (
            getattr(s, self.name + "_" + kind) for kind in ("got", "part", "got2", "sum", "send", "recv")
        )
        self.c = coords(me)[3]
        self.p = self.first[1](me, 0)[1]
        self.q = self.second[1](me, 0)[1]

    def copy(self, phase, src, dst, d, to):
        return remote(src, dst, self.send.at[phase, d], self.recv.at[phase, d], to)

    def scatter(self, d):
        to, q = self.first[1](self.me, d)
        return self.copy(0, self.w.at[pl.ds(self.start + q * self.per, self.per)], self.got.at[d], d, to)

    def scatter2(self, d):
        to, q = self.second[1](self.me, d)
        return self.copy(1, self.part.at[pl.ds(q, 1)], self.got2.at[d], d, to)

    def gather2(self, d):
        to, q = self.second[1](self.me, d)
        here = self.sum.at[pl.ds(self.q, 1)]
        return self.copy(2, here, here, d, to)

    def piece(self, q):
        return self.out.at[self.c, pl.ds(self.start + q * self.per, self.per)]

    def gather(self, d):
        to, q = self.first[1](self.me, d)
        return self.copy(3, self.sum.at[pl.ds(0, self.per)], self.piece(self.p), d, to)

    def own(self):
        return pltpu.make_async_copy(self.sum.at[pl.ds(0, self.per)], self.piece(self.p), self.send.at[3, 0])

    def hand(self, d):
        here = self.piece(self.first[2](self.me, d))
        return self.copy(4, here, here, d, other_core(self.me))

    def start_scatter(self):
        each(1, self.first[0], lambda d: self.scatter(d).start())

    def start_scatter2(self):
        each(1, self.first[0], lambda d: self.scatter(d).wait_recv())

        def add(i):
            total = self.w[self.start + self.p * self.per + i].astype(F32)
            total += jnp.sum(self.got[1:, i].astype(F32), axis=0)
            self.part[i] = total.astype(BF16)

        each(0, self.per, add)
        m = self.second[0]
        if m > self.per:
            self.part[self.per:] = jnp.zeros((m - self.per, 16, 128), BF16)
        each(1, m, lambda d: self.scatter2(d).start())

    def start_gather2(self):
        m = self.second[0]
        each(1, m, lambda d: self.scatter2(d).wait_recv())
        total = self.part[self.q].astype(F32) + jnp.sum(self.got2[1:, 0].astype(F32), axis=0)
        self.sum[self.q] = total.astype(BF16)
        each(1, m, lambda d: self.gather2(d).start())

    def start_gather(self):
        each(1, self.second[0], lambda d: self.gather2(d).wait_recv())
        each(1, self.first[0], lambda d: self.gather(d).start())
        self.own().start()

    def pass_own(self):
        self.own().wait()
        self.hand(0).start()

    def pass_on(self):
        def move(d):
            self.gather(d).wait_recv()
            self.hand(d).start()

        each(1, self.first[0], move)

    def finish(self):
        n, m = self.first[0], self.second[0]
        each(1, n, lambda d: self.scatter(d).wait_send())
        each(1, m, lambda d: self.scatter2(d).wait_send())
        each(1, m, lambda d: self.gather2(d).wait_send())
        each(1, n, lambda d: self.gather(d).wait_send())
        each(0, n, lambda d: self.hand(d).wait())


def streams():
    return (
        Stream("a1", 0, 7, XY_AXIS, Z_AXIS),
        Stream("b1", 112, 6, Z_AXIS, XY_AXIS),
        Stream("a2", 160, 7, XY_AXIS, Z_AXIS),
        Stream("b2", 272, 7, Z_AXIS, XY_AXIS),
    )


def greet_all(me):
    barrier = pltpu.get_barrier_semaphore()

    def greet(to):
        pl.semaphore_signal(barrier, inc=1, device_id=(to,), device_id_type=MESH)

    greet(far_device(me))
    greet(other_core(me))
    each(1, XY, lambda d: greet(xy_member(me, d)[0]))
    each(1, ZS, lambda d: greet(z_member(me, d)[0]))
    return barrier


RC = 128
EARLY = 320
NC = ROWS // RC
CW = 384
TAIL = 256
HB = 288


def rows_at(start, size):
    return pl.ds(pl.multiple_of(start, size), size)


def dot_nt(a, b):
    return lax.dot_general(a, b, (((1,), (1,)), ((), ())), preferred_element_type=F32)


def dot_nn(a, b):
    return jnp.dot(a, b, preferred_element_type=F32)


def unit_of(values):
    rinv = lax.rsqrt(jnp.sum(values * values, axis=-1, keepdims=True) + 1e-06)
    return (values * rinv, rinv)


def own_diagonal(shape):
    row = lax.broadcasted_iota(jnp.int32, shape, 0)
    return lax.broadcasted_iota(jnp.int32, shape, 1) == row


def across(total, unit, rinv):
    along = jnp.sum(unit * total, axis=-1, keepdims=True)
    return ((total - unit * along) * rinv).astype(BF16)


def main_kernel(img_hbm, feat_hbm, head_hbm, scale_ref, bias_ref, tiles, txt_out, img_out, *scratch):
    me = lax.axis_index("batch")
    c = me % CS
    near = other_core(me)
    far = far_device(me)
    s = Names()
    for name, ref in zip(list(MAIN_SCRATCH), scratch):
        setattr(s, name, ref)
    a1, b1, a2, b2 = lines = streams()
    for line in lines:
        line.bind(me, s.w, tiles, s)
    img_in = pltpu.make_async_copy(img_hbm, s.img, s.ins.at[0])
    feat_in = pltpu.make_async_copy(feat_hbm, s.feat, s.ins.at[1])
    head_in = pltpu.make_async_copy(head_hbm, s.head, s.ins.at[2])
    img_in.start()
    feat_in.start()
    head_in.start()
    barrier = greet_all(me)
    half = 0.5 * jnp.exp(jnp.full((1, 1), scale_ref[0], F32))
    shift = 0.5 * jnp.full((1, 1), bias_ref[0], F32)

    def weights(left, right, diagonal=False):
        weight = jnp.tanh(dot_nt(left, right) * half + shift) * half + half
        if diagonal:
            weight = weight - jnp.where(own_diagonal(weight.shape), 2.0 * half, 0.0)
        return weight.astype(BF16)

    def img_far(j):
        start, size = ((0, 2 * RC), (2 * RC, RC), (3 * RC, RC))[j]
        return remote(s.imgs.at[pl.ds(start, size)], s.imgs.at[pl.ds(2 * ROWS + start, size)],
                      s.es.at[j], s.er.at[j], far)

    def txt_far(j):
        start, size = ((0, EARLY), (EARLY, ROWS - EARLY))[j]
        return remote(s.txts.at[pl.ds(start, size)], s.txts.at[pl.ds(2 * ROWS + start, size)],
                      s.es.at[NC + j], s.er.at[NC + j], far)

    n = 2 * NC
    img_near = remote(s.imgs.at[pl.ds(0, ROWS)], s.imgs.at[pl.ds(ROWS, ROWS)], s.es.at[n], s.er.at[n], near)
    txt_near = remote(s.txts.at[pl.ds(0, ROWS)], s.txts.at[pl.ds(ROWS, ROWS)], s.es.at[n + 1], s.er.at[n + 1], near)
    theirs = rows_at((1 - c) * HALF, HALF)
    feat_near = remote(s.feat_t.at[theirs], s.feat_nbr, s.es.at[n + 2], s.er.at[n + 2], near)

    def hid_near(k):
        return remote(s.hid.at[pl.ds(k * TAIL, TAIL)], s.hid.at[pl.ds(ROWS + k * TAIL, TAIL)],
                      s.es.at[n + 3 + k], s.er.at[n + 3 + k], near)

    img_in.wait()

    def unit_images(j):
        at = pl.ds(j * RC, RC)
        unit, rinv = unit_of(s.img[at, :].astype(F32))
        s.imgs[at, :] = unit.astype(BF16)
        s.img_rinv[at, :] = rinv

    unit_images(0)
    unit_images(1)
    pl.semaphore_wait(barrier, XY + ZS)
    img_far(0).start()
    unit_images(2)
    img_far(1).start()
    unit_images(3)
    img_far(2).start()
    img_near.start()
    feat_in.wait()
    head_in.wait()
    s.txt_unit[...] = dot_nn(s.feat[...], s.head[...])

    def unit_texts(j):
        at = rows_at(j * RC, RC)
        unit, rinv = unit_of(s.txt_unit[at, :])
        s.txt_unit[at, :] = unit
        s.txts[at, :] = unit.astype(BF16)
        s.txt_rinv[at, :] = rinv

    each(0, NC, unit_texts)
    txt_near.start()
    txt_far(0).start()

    own = pl.ds(0, ROWS)
    nbr = pl.ds(ROWS, ROWS)
    s.wt[:, 0:ROWS] = weights(s.txts[own, :], s.imgs[own, :], True)

    def flip(i):
        cols = rows_at(i * 128, 128)
        s.feat_t[cols, :] = s.feat[:, cols].T

    each(0, COLS, flip)
    feat_near.start()
    img_near.wait_recv()
    s.wt[:, ROWS:2 * ROWS] = weights(s.txts[own, :], s.imgs[nbr, :])

    def sums_of(sums, block, first, size, add):
        def columns(i):
            cols = rows_at(i * CW, CW)
            value = dot_nn(s.wt[:, first:first + size], block[first:first + size, cols])
            sums[:, cols] = sums[:, cols] + value if add else value

        each(0, E // CW, columns)

    sums_of(s.text_sum, s.imgs, 0, 2 * ROWS, False)
    base = 2 * ROWS
    img_far(0).wait_recv()
    s.wt[:, base:base + 2 * RC] = weights(s.txts[own, :], s.imgs[pl.ds(base, 2 * RC), :])
    img_far(1).wait_recv()
    s.wt[:, base + 2 * RC:base + 3 * RC] = weights(s.txts[own, :], s.imgs[pl.ds(base + 2 * RC, RC), :])
    sums_of(s.text_sum, s.imgs, base, 3 * RC, True)
    img_far(2).wait_recv()
    last = pl.ds(base + 3 * RC, RC)
    for k in range(ROWS // TAIL):
        at = pl.ds(k * TAIL, TAIL)
        weight = weights(s.txts[at, :], s.imgs[last, :])
        total = s.text_sum[at, :] + dot_nn(weight, s.imgs[last, :])
        s.hid[at, :] = across(total, s.txt_unit[at, :], s.txt_rinv[at, :])
        hid_near(k).start()

    def head_own(i):
        mine = s.feat_t[rows_at(c * HALF + i * HB, HB), :]
        s.head_sum[rows_at(i * HB, HB), :] = dot_nn(mine, s.hid[own, :])

    each(0, HALF // HB, head_own)
    feat_near.wait_recv()
    for k in range(ROWS // TAIL):
        hid_near(k).wait_recv()

    def head_both(i):
        at = pl.ds(i * HB, HB)
        value = s.head_sum[at, :] + dot_nn(s.feat_nbr[at, :], s.hid[nbr, :])
        value = value.astype(BF16)
        for r in range(HB // 16):
            for col in range(COLS):
                s.w[(i * HB // 16 + r) * COLS + col] = value[r * 16:(r + 1) * 16, col * 128:(col + 1) * 128]

    head_both(0)
    a1.start_scatter()
    b1.start_scatter()
    head_both(1)
    s.w[UNITS * COLS:] = jnp.zeros((NT - UNITS * COLS, 16, 128), BF16)
    a2.start_scatter()
    b2.start_scatter()

    txt_write = pltpu.make_async_copy(s.txt_grad, txt_out, s.outs.at[0])
    img_write = pltpu.make_async_copy(s.img_grad, img_out, s.outs.at[1])

    def text_grads(i):
        cols = rows_at(i * CW, CW)
        s.txt_grad[:, cols] = dot_nt(s.hid[own, :], s.head[cols, :]).astype(BF16)

    each(0, E // CW, text_grads)
    txt_write.start()
    s.wt[:, 0:ROWS] = weights(s.imgs[own, :], s.txts[own, :], True)
    txt_near.wait_recv()
    s.wt[:, ROWS:2 * ROWS] = weights(s.imgs[own, :], s.txts[nbr, :])
    b1.start_scatter2()
    sums_of(s.img_sum, s.txts, 0, 2 * ROWS, False)
    a1.start_scatter2()

    def image_far(j):
        start, size = ((0, EARLY), (EARLY, ROWS - EARLY))[j]
        txt_far(j).wait_recv()
        s.wt[:, base + start:base + start + size] = weights(s.imgs[own, :], s.txts[pl.ds(base + start, size), :])
        sums_of(s.img_sum, s.txts, base + start, size, True)

    image_far(0)

    for line in (b2, a2):
        line.start_scatter2()
    txt_far(1).start()
    for line in (b1, a1, b2, a2):
        line.start_gather2()
    for line in (b1, a1, b2, a2):
        line.start_gather()
    for line in (b1, a1, b2, a2):
        line.pass_own()
    b1.pass_on()
    a1.pass_on()
    image_far(1)
    def image_grads(j):
        at = rows_at(j * RC, RC)
        rinv = s.img_rinv[at, :]
        s.img_grad[at, :] = across(s.img_sum[at, :], s.img[at, :].astype(F32) * rinv, rinv)

    each(0, NC, image_grads)
    img_write.start()
    b2.pass_on()
    a2.pass_on()
    for line in lines:
        line.finish()
    for j in range(3):
        img_far(j).wait_send()
    for j in range(2):
        txt_far(j).wait_send()
    img_near.wait_send()
    txt_near.wait_send()
    feat_near.wait_send()
    for k in range(ROWS // TAIL):
        hid_near(k).wait_send()
    txt_write.wait()
    img_write.wait()


MAIN_SCRATCH = dict(
    img=pltpu.VMEM((ROWS, E), BF16),
    feat=pltpu.VMEM((ROWS, E), BF16),
    head=pltpu.VMEM((E, E), BF16),
    imgs=pltpu.VMEM((3 * ROWS, E), BF16),
    txts=pltpu.VMEM((3 * ROWS, E), BF16),
    wt=pltpu.VMEM((ROWS, 3 * ROWS), BF16),
    img_rinv=pltpu.VMEM((ROWS, 1), F32),
    txt_rinv=pltpu.VMEM((ROWS, 1), F32),
    txt_unit=pltpu.VMEM((ROWS, E), F32),
    text_sum=pltpu.VMEM((ROWS, E), F32),
    img_sum=pltpu.VMEM((ROWS, E), F32),
    hid=pltpu.VMEM((2 * ROWS, E), BF16),
    feat_t=pltpu.VMEM((E, ROWS), BF16),
    feat_nbr=pltpu.VMEM((HALF, ROWS), BF16),
    head_sum=pltpu.VMEM((HALF, E), F32),
    w=pltpu.VMEM((NT, 16, 128), BF16),
    txt_grad=pltpu.VMEM((ROWS, E), BF16),
    img_grad=pltpu.VMEM((ROWS, E), BF16),
    ins=pltpu.SemaphoreType.DMA((3,)),
    outs=pltpu.SemaphoreType.DMA((2,)),
    es=pltpu.SemaphoreType.DMA((2 * NC + 5,)),
    er=pltpu.SemaphoreType.DMA((2 * NC + 5,)),
)
for line in streams():
    MAIN_SCRATCH.update(line.scratch())


def main_call(img_emb, txt_feat, txt_head, log_scale, bias):
    return pl.pallas_call(
        main_kernel,
        out_shape=(
            jax.ShapeDtypeStruct((CS, NT, 16, 128), BF16),
            jax.ShapeDtypeStruct((ROWS, E), BF16),
            jax.ShapeDtypeStruct((ROWS, E), BF16),
        ),
        in_specs=[pl.BlockSpec(memory_space=pl.ANY)] * 3 + [pl.BlockSpec(memory_space=pltpu.SMEM)] * 2,
        out_specs=[pl.BlockSpec(memory_space=pl.ANY)] * 3,
        scratch_shapes=list(MAIN_SCRATCH.values()),
        compiler_params=pltpu.CompilerParams(
            collective_id=0, has_side_effects=True, vmem_limit_bytes=56 << 20
        ),
        name="main",
    )(img_emb, txt_feat, txt_head, log_scale, bias)


LAY = 288


def final_kernel(tiles_hbm, txt_hbm, img_hbm, head_out, txt_out, img_out, tiles, head, txt, img, sems):
    txt_in = pltpu.make_async_copy(txt_hbm, txt, sems.at[0])
    img_in = pltpu.make_async_copy(img_hbm, img, sems.at[1])
    txt_back = pltpu.make_async_copy(txt, txt_out, sems.at[2])
    img_back = pltpu.make_async_copy(img, img_out, sems.at[3])
    per = LAY // 16 * COLS
    blocks = HALF // LAY

    def read(i):
        at = pl.ds((i % blocks) * per, per)
        return pltpu.make_async_copy(tiles_hbm.at[i // blocks, at], tiles.at[i // blocks, at], sems.at[4 + i])

    def write(i):
        at = rows_at(i * LAY, LAY)
        return pltpu.make_async_copy(head.at[at], head_out.at[at], sems.at[4 + CS * blocks + i])

    each(0, CS * blocks, lambda i: read(i).start())
    txt_in.start()
    img_in.start()

    def lay(i):
        read(i).wait()
        for r in range(LAY // 16):
            for col in range(COLS):
                value = tiles[i // blocks, (i % blocks) * per + r * COLS + col]
                head[pl.ds(pl.multiple_of(i * LAY + r * 16, 16), 16), col * 128:(col + 1) * 128] = value.astype(F32)
        write(i).start()

    each(0, CS * blocks, lay)
    txt_in.wait()
    txt_back.start()
    img_in.wait()
    img_back.start()
    each(0, CS * blocks, lambda i: write(i).wait())
    txt_back.wait()
    img_back.wait()


def final_call(tiles, txt_grad, img_grad):
    return pl.pallas_call(
        final_kernel,
        out_shape=(
            jax.ShapeDtypeStruct((E, E), F32),
            jax.ShapeDtypeStruct((ROWS, E), BF16),
            jax.ShapeDtypeStruct((ROWS, E), BF16),
        ),
        in_specs=[pl.BlockSpec(memory_space=pl.ANY)] * 3,
        out_specs=[pl.BlockSpec(memory_space=pl.ANY)] * 3,
        scratch_shapes=[
            pltpu.VMEM((CS, NT, 16, 128), BF16),
            pltpu.VMEM((E, E), F32),
            pltpu.VMEM((ROWS, E), BF16),
            pltpu.VMEM((ROWS, E), BF16),
            pltpu.SemaphoreType.DMA((4 + 2 * CS * HALF // LAY,)),
        ],
        compiler_params=pltpu.CompilerParams(vmem_limit_bytes=56 << 20),
        name="final",
    )(tiles, txt_grad, img_grad)


def shards(img_emb, txt_feat, txt_head, log_scale, bias):
    tiles, txt_grad, img_grad = main_call(img_emb, txt_feat, txt_head, log_scale, bias)
    head_grad, txt_grad, img_grad = final_call(tiles, txt_grad, img_grad)
    return (img_grad, txt_grad, head_grad)


def solution(mesh):
    return jax.shard_map(
        shards,
        mesh=mesh,
        in_specs=(P("batch", None), P("batch", None), P(), P(), P()),
        out_specs=(P("batch", None), P("batch", None), P()),
        check_vma=False,
    )
```
